32 devices in a mesh: fsdp: 8 (over z, x), tensor: 4 (over y, core).
Axes of the slice: x: 2, y: 2, z: 4, core: 2. Of those that a mesh axis runs over, the one named last changes fastest.
Arguments:
- tokens: bfloat16 [6144, 5120], P('fsdp', 'tensor'), may hold values from -48 to 48
- live_rows: int32 [8], P('fsdp'), may hold values from 128 to 768, as said below
- first_row: int32 [6144], P('fsdp'), may hold values from 0 to 767, as said below
- w_query: bfloat16 [5120, 2560], P('fsdp', 'tensor'), may hold values from -1 to 1
- w_key: bfloat16 [5120, 512], P('fsdp', 'tensor'), may hold values from -1 to 1
- w_value: bfloat16 [5120, 512], P('fsdp', 'tensor'), may hold values from -0.078125 to 0.078125
- w_out: bfloat16 [2560, 5120], P('tensor', 'fsdp'), may hold values from -1 to 1
- query_gain: float32 [2560], P('tensor'), may hold values from 0.5 to 1.5
- key_gain: float32 [512], P('tensor'), may hold values from 0.5 to 1.5
- out_gain: float32 [5120], P('tensor'), may hold values from 0.5 to 1.5
Outputs:
- output: bfloat16 [6144, 5120], P('fsdp', 'tensor')
The draws below stay inside these ranges and needn't reach their ends.
Inputs may be any that keep to these rules, and one draw needn't show every extreme that they name: `live_rows`: each entry is a multiple of 128; the largest value is reached on some index of every draw. `first_row`: each row's value is never above its own local index and never below the first local index of its pack (384 rows); the last row of each block begins a document of one row.
All inputs are finite; a program needn't handle non-finite values.
Results may differ from the reference program's by a relative error of at most 0.009.
Values may be sent and summed in bfloat16 or wider, within the bound.
No kernel may reach another device: no remote copies, remote signals or barrier semaphores. Data moves between devices by JAX's collectives and lax.ppermute only.
A program may use at most 128 MiB of HBM per device.

```python
import math
import jax
import jax.numpy as jnp
from jax import lax

D = 5120
HEADS = 20
KV_HEADS = 4
HEAD_DIM = 128
BLOCK = 128
CAP = 768
HALF = 384
TOKENS = 6144
N_FSDP = 8
N_TENSOR = 4


def draw_tokens(key, part):
    values = jnp.clip(jax.random.normal(jax.random.fold_in(key, 1), (TOKENS, D), jnp.float32), -6.0, 6.0)
    return values.astype(jnp.bfloat16)


def draw_live_rows(key, part):
    devices = TOKENS // CAP
    total_blocks = CAP // BLOCK
    index = jnp.arange(devices, dtype=jnp.int32)
    base = total_blocks - index * (total_blocks - 1) // max(devices - 1, 1)
    jitter = jax.random.randint(jax.random.fold_in(key, 3), (devices,), 0, 2, dtype=jnp.int32)
    blocks = jnp.where(index == 0, total_blocks, jnp.maximum(base - jitter, 1))
    return (blocks * BLOCK).astype(jnp.int32)


def draw_first_row(key, part):
    devices = TOKENS // CAP
    local = jnp.arange(CAP, dtype=jnp.int32)[None, :]
    marks = jax.random.randint(jax.random.fold_in(key, 4), (devices, CAP), 0, 200, dtype=jnp.int32) == 0
    cuts = jax.random.randint(jax.random.fold_in(key, 5), (devices, 2), 1, CAP // 2, dtype=jnp.int32)
    marks = marks | (local % (CAP // 2) == 0) | (local == cuts[:, :1]) | (local == cuts[:, 1:] + CAP // 2)
    marks = marks | (local == CAP - 1)
    starts = lax.cummax(jnp.where(marks, local, 0), axis=1)
    return starts.reshape(TOKENS).astype(jnp.int32)


def draw_w_query(key, part):
    scale = jnp.power(3.0, jnp.repeat(jnp.arange(HEADS, dtype=jnp.float32), HEAD_DIM) / (HEADS - 1))
    noise = jax.random.normal(jax.random.fold_in(key, 6), (D, HEADS * HEAD_DIM), jnp.float32) / math.sqrt(D)
    return jnp.clip(noise * scale[None, :], -1.0, 1.0).astype(jnp.bfloat16)


def draw_w_key(key, part):
    scale = jnp.power(3.0, jnp.repeat(jnp.arange(KV_HEADS, dtype=jnp.float32), HEAD_DIM) / (KV_HEADS - 1))
    noise = jax.random.normal(jax.random.fold_in(key, 7), (D, KV_HEADS * HEAD_DIM), jnp.float32) / math.sqrt(D)
    return jnp.clip(noise * scale[None, :], -1.0, 1.0).astype(jnp.bfloat16)


def draw_w_out(key, part):
    scale = jnp.power(3.0, jnp.arange(D, dtype=jnp.float32) / (D - 1))
    fan = math.sqrt(HEADS * HEAD_DIM)
    noise = jax.random.normal(jax.random.fold_in(key, 8), (HEADS * HEAD_DIM, D), jnp.float32)
    return jnp.clip(noise * scale[None, :] / fan, -1.0, 1.0).astype(jnp.bfloat16)


def draw_query_gain(key, part):
    return jax.random.uniform(jax.random.fold_in(key, 9), (HEADS * HEAD_DIM,), jnp.float32, 0.5, 1.5)


def draw_key_gain(key, part):
    return jax.random.uniform(jax.random.fold_in(key, 10), (KV_HEADS * HEAD_DIM,), jnp.float32, 0.5, 1.5)


def block_levels(stream_key, shape, cuts, least, top_value):
    factor_of = 1.0
    for position, shards_of in cuts:
        draws = jax.random.uniform(jax.random.fold_in(jax.random.fold_in(stream_key, 6), position), (shards_of,), jnp.float32, least / len(cuts), top_value / len(cuts))
        factor_of = factor_of * jnp.repeat(jnp.exp(draws), shape[position] // shards_of).reshape((-1,) + (1,) * (len(shape) - 1 - position))
    return factor_of


def centred(key, extent, spread, most, pieces=(), kind=jnp.bfloat16):
    array = spread * jax.random.normal(key, extent, jnp.float32)
    if pieces:
        array = array * block_levels(key, extent, pieces, -0.22, 0.18)
    return jnp.clip(array, -most, most).astype(kind)


def setup_inputs(seed: int = 0) -> dict:
    splits = jax.random.split(jax.random.key(seed), 11)
    return {
        "tokens": draw_tokens(jax.random.fold_in(splits[10], 71), 0),
        "live_rows": draw_live_rows(jax.random.fold_in(splits[10], 71), 0),
        "first_row": draw_first_row(jax.random.fold_in(splits[10], 71), 0),
        "w_query": draw_w_query(jax.random.fold_in(splits[10], 71), 0),
        "w_key": draw_w_key(jax.random.fold_in(splits[10], 71), 0),
        "w_value": centred(splits[5], (D, KV_HEADS * HEAD_DIM), D ** -0.5, 0.078125, ((0, 8), (1, 4))),
        "w_out": draw_w_out(jax.random.fold_in(splits[10], 71), 0),
        "query_gain": draw_query_gain(jax.random.fold_in(splits[10], 71), 0),
        "key_gain": draw_key_gain(jax.random.fold_in(splits[10], 71), 0),
        "out_gain": jnp.clip(0.5 + 1.0 * jax.random.uniform(splits[9], (D,), jnp.float32) ** block_levels(splits[9], (D,), ((0, 4),), -0.2, 0.2), 0.5, 1.5),
    }


EPS = 1e-06
ROPE_BASE = 500000.0

def rotate(field, positions):
    half_dim = field.shape[-1] // 2
    freqs = jnp.power(ROPE_BASE, -(jnp.arange(half_dim, dtype=jnp.float32) * 2.0 / field.shape[-1]))
    angle = positions[:, None] * freqs[None, :]
    cosine = jnp.cos(angle)[:, None, :]
    sine_part = jnp.sin(angle)[:, None, :]
    first = field[..., :half_dim]
    second = field[..., half_dim:]
    return jnp.concatenate([first * cosine - second * sine_part, second * cosine + first * sine_part], axis=-1)

def attend(queries, keys, values, starts, offset):
    row_count = queries.shape[0]
    kv_count = keys.shape[1]
    group_size = queries.shape[1] // kv_count
    grouped = queries.reshape(row_count, kv_count, group_size, HEAD_DIM).astype(jnp.float32)
    scores = jnp.einsum('qkgd,skd->kgqs', grouped, keys.astype(jnp.float32)) / math.sqrt(HEAD_DIM)
    local = jnp.arange(row_count, dtype=jnp.int32)
    allowed = (local[None, :] >= (starts - offset)[:, None]) & (local[None, :] <= local[:, None])
    scores = jnp.where(allowed[None, None], scores, jnp.float32(-1e+30))
    peak_value = lax.optimization_barrier(jnp.max(scores, axis=-1, keepdims=True))
    expo = jnp.exp(scores - peak_value)
    totals = lax.optimization_barrier(jnp.sum(expo, axis=-1, keepdims=True))
    probs = (expo / totals).astype(jnp.bfloat16)
    mixed = jnp.einsum('kgqs,skd->qkgd', probs.astype(jnp.float32), values.astype(jnp.float32))
    return mixed.reshape(row_count, -1).astype(jnp.bfloat16)

def reference(tokens, live_rows, first_row, w_query, w_key, w_value, w_out, query_gain, key_gain, out_gain):
    blocks = tokens.reshape(N_FSDP, CAP, D)
    offsets = first_row.reshape(N_FSDP, CAP)

    def layer(items):
        inputs, live_count, starts = items
        query = jnp.dot(inputs, w_query, preferred_element_type=jnp.float32)
        key = jnp.dot(inputs, w_key, preferred_element_type=jnp.float32)
        value = jnp.dot(inputs, w_value, preferred_element_type=jnp.float32).astype(jnp.bfloat16)
        query_normed = query * lax.rsqrt(lax.optimization_barrier(jnp.mean(query * query, axis=1, keepdims=True)) + EPS) * query_gain
        key_normed = key * lax.rsqrt(lax.optimization_barrier(jnp.mean(key * key, axis=1, keepdims=True)) + EPS) * key_gain
        row_ids = jnp.arange(CAP, dtype=jnp.int32)
        positions = (row_ids - starts).astype(jnp.float32)
        query_rot = rotate(query_normed.reshape(CAP, HEADS, HEAD_DIM), positions).astype(jnp.bfloat16)
        key_rot = rotate(key_normed.reshape(CAP, KV_HEADS, HEAD_DIM), positions).astype(jnp.bfloat16)
        value_heads = value.reshape(CAP, KV_HEADS, HEAD_DIM)
        packs = []
        for pack_index in range(2):
            lower = pack_index * HALF
            packs.append(attend(query_rot[lower:lower + HALF], key_rot[lower:lower + HALF], value_heads[lower:lower + HALF], starts[lower:lower + HALF], lower))
        attended = jnp.concatenate(packs, axis=0)
        width = HEADS * HEAD_DIM // N_TENSOR
        attn_out = jnp.zeros((CAP, D), jnp.float32)
        for group in range(N_TENSOR):
            partial_value = jnp.dot(attended[:, group * width:(group + 1) * width], w_out[group * width:(group + 1) * width], preferred_element_type=jnp.float32).astype(jnp.bfloat16)
            partial_value = lax.optimization_barrier(partial_value)
            attn_out = attn_out + partial_value.astype(jnp.float32)
        scale = lax.rsqrt(lax.optimization_barrier(jnp.mean(attn_out * attn_out, axis=1, keepdims=True)) + EPS)
        result = (inputs.astype(jnp.float32) + attn_out * scale * out_gain).astype(jnp.bfloat16)
        return jnp.where((row_ids < live_count)[:, None], result, jnp.zeros_like(result))
    outputs = lax.map(layer, (blocks, live_rows, offsets))
    return outputs.reshape(TOKENS, D)
```

```python
import math

import jax
import jax.numpy as jnp
from jax import lax
from jax.sharding import PartitionSpec as P

HEAD_DIM = 128
EPS = 1e-06
ROPE_BASE = 500000.0
AXES = ("fsdp", "tensor")


def permute(array, mesh_sizes, target):
    n, tensor_size = mesh_sizes
    pairs = []
    for f in range(n):
        for t in range(tensor_size):
            to_f, to_t = target(f, t)
            pairs.append((f * tensor_size + t, to_f * tensor_size + to_t))
    return lax.ppermute(array, AXES, pairs)


def reverse_bits(value, size):
    result = 0
    while size > 1:
        result = result * 2 + value % 2
        value //= 2
        size //= 2
    return result


def snake(n):
    return list(range(0, n, 2)) + list(range(n - 1, 0, -2))


def gather_tensor(array, sizes):
    have = {0: array}
    bit = sizes[1] // 2
    while bit:
        for r in sorted(have):
            have[r ^ bit] = permute(have[r], sizes, lambda f, t, bit=bit: (f, t ^ bit))
        bit //= 2
    return [have[r] for r in range(sizes[1])]


def ring_gather(top, bottom, sizes):
    n = sizes[0]
    order = snake(n)
    place = {f: i for i, f in enumerate(order)}
    tops, bottoms = [top], [bottom]
    for _ in range(n - 1):
        tops.append(permute(tops[-1], sizes, lambda f, t: (order[(place[f] + 1) % n], t)))
        bottoms.append(permute(bottoms[-1], sizes, lambda f, t: (order[(place[f] - 1) % n], t)))
    return tops, bottoms


def rotate(field, cosine, sine):
    half_dim = field.shape[-1] // 2
    first = field[..., :half_dim]
    second = field[..., half_dim:]
    return jnp.concatenate([first * cosine - second * sine, second * cosine + first * sine], axis=-1)


def attend(queries, keys, values, starts, offset):
    row_count = queries.shape[0]
    kv_count = keys.shape[1]
    group_size = queries.shape[1] // kv_count
    grouped = queries.reshape(row_count, kv_count, group_size, HEAD_DIM)
    scores = jnp.einsum(
        "qkgd,skd->kgqs", grouped, keys, preferred_element_type=jnp.float32
    ) / math.sqrt(HEAD_DIM)
    local = jnp.arange(row_count, dtype=jnp.int32)
    allowed = (local[None, :] >= (starts - offset)[:, None]) & (local[None, :] <= local[:, None])
    scores = jnp.where(allowed[None, None], scores, jnp.float32(-1e30))
    peak_value = jnp.max(scores, axis=-1, keepdims=True)
    expo = jnp.exp(scores - peak_value)
    totals = jnp.sum(expo, axis=-1, keepdims=True)
    probs = (expo / totals).astype(jnp.bfloat16)
    mixed = jnp.einsum("kgqs,skd->qkgd", probs, values, preferred_element_type=jnp.float32)
    return mixed.reshape(row_count, -1).astype(jnp.bfloat16)


def body(
    sizes, tokens, live_rows, first_row, w_query, w_key, w_value, w_out, query_gain, key_gain, out_gain
):
    n, tensor_size = sizes
    capacity, width = tokens.shape
    half_rows = capacity // 2
    per_tensor = n // tensor_size
    f_index = lax.axis_index("fsdp")
    t_index = lax.axis_index("tensor")
    order = snake(n)
    place = [order.index(f) for f in range(n)]
    order_of = jnp.array(order, jnp.int32)
    position = jnp.array(place, jnp.int32)[f_index]

    weights = jnp.concatenate([w_query, w_key, w_value], axis=1)
    depth = weights.shape[0]
    half = depth // 2
    token_blocks = gather_tensor(tokens, sizes)
    tops, bottoms = ring_gather(weights[:half], weights[half:], sizes)

    moved = permute(
        w_out,
        sizes,
        lambda f, t: (
            ((f // per_tensor) ^ reverse_bits(t, tensor_size)) * per_tensor + f % per_tensor,
            t,
        ),
    )
    moved = permute(
        moved, sizes, lambda f, t: (f, (f // per_tensor) ^ reverse_bits(t, tensor_size))
    )

    token_stack = jnp.stack(token_blocks)
    total = None
    steps = [(0, n // 2)] + [(s, n - s) for s in range(n // 2 + 1, n)]
    for group in steps:
        for offset in group:
            block = order_of[lax.rem(position + offset, n)]
            relative = (block // per_tensor) ^ t_index
            piece = lax.dynamic_slice(
                token_stack, (relative, 0, lax.rem(block, per_tensor) * depth), (1, capacity, depth)
            )[0]
            matrix = jnp.concatenate([tops[(n - offset) % n], bottoms[offset]], axis=0)
            term = jnp.dot(piece, matrix, preferred_element_type=jnp.float32)
            total = term if total is None else total + term

    out_top, out_bottom, total = lax.optimization_barrier(
        (moved[: w_out.shape[0] // 2], moved[w_out.shape[0] // 2 :], total)
    )
    out_tops, out_bottoms = ring_gather(out_top, out_bottom, sizes)

    q_width, k_width = w_query.shape[1], w_key.shape[1]
    query = total[:, :q_width]
    key = total[:, q_width : q_width + k_width]
    value = total[:, q_width + k_width :]
    query_sq, key_sq = lax.psum(
        (jnp.sum(query * query, axis=1), jnp.sum(key * key, axis=1)), "tensor"
    )
    query_normed = (
        query * lax.rsqrt(query_sq / (q_width * tensor_size) + EPS)[:, None] * query_gain
    )
    key_normed = key * lax.rsqrt(key_sq / (k_width * tensor_size) + EPS)[:, None] * key_gain
    row_ids = jnp.arange(capacity, dtype=jnp.int32)
    positions = (row_ids - first_row).astype(jnp.float32)
    half_dim = HEAD_DIM // 2
    freqs = jnp.power(
        ROPE_BASE, -(jnp.arange(half_dim, dtype=jnp.float32) * 2.0 / HEAD_DIM)
    )
    angle = positions[:, None] * freqs[None, :]
    cosine = jnp.cos(angle)[:, None, :]
    sine = jnp.sin(angle)[:, None, :]
    query_rot = rotate(query_normed.reshape(capacity, -1, HEAD_DIM), cosine, sine).astype(jnp.bfloat16)
    key_rot = rotate(key_normed.reshape(capacity, -1, HEAD_DIM), cosine, sine).astype(jnp.bfloat16)
    value_heads = value.astype(jnp.bfloat16).reshape(capacity, -1, HEAD_DIM)
    packs = []
    for pack_index in range(2):
        lower = pack_index * half_rows
        packs.append(
            attend(
                query_rot[lower : lower + half_rows],
                key_rot[lower : lower + half_rows],
                value_heads[lower : lower + half_rows],
                first_row[lower : lower + half_rows],
                lower,
            )
        )
    attended = jnp.concatenate(packs, axis=0)
    attended_stack = jnp.stack(gather_tensor(attended, sizes))

    reversed_of = jnp.array(
        [reverse_bits(t, tensor_size) for t in range(tensor_size)], jnp.int32
    )
    result = jnp.zeros((per_tensor, capacity, w_out.shape[1]), jnp.float32)
    for group in steps:
        for offset in group:
            block = order_of[lax.rem(position + offset, n)]
            source = reversed_of[(block // per_tensor) ^ t_index]
            column = lax.rem(block, per_tensor)
            piece = lax.dynamic_index_in_dim(attended_stack, source ^ t_index, 0, False)
            matrix = jnp.concatenate([out_tops[(n - offset) % n], out_bottoms[offset]], axis=0)
            term = jnp.dot(piece, matrix, preferred_element_type=jnp.float32)
            current = lax.dynamic_index_in_dim(result, column, 0, False)
            result = lax.dynamic_update_index_in_dim(result, current + term, column, 0)
    attn_out = jnp.concatenate([result[q] for q in range(per_tensor)], axis=1)

    out_sq = lax.psum(jnp.sum(attn_out * attn_out, axis=1), "tensor")
    scale = lax.rsqrt(out_sq / (width * tensor_size) + EPS)[:, None]
    summed = (tokens.astype(jnp.float32) + attn_out * scale * out_gain).astype(jnp.bfloat16)
    return jnp.where((row_ids < live_rows[0])[:, None], summed, jnp.zeros_like(summed))


def solution(mesh):
    sizes = (mesh.shape["fsdp"], mesh.shape["tensor"])

    def run(*arrays):
        return body(sizes, *arrays)

    in_specs = (
        P("fsdp", "tensor"),
        P("fsdp"),
        P("fsdp"),
        P("fsdp", "tensor"),
        P("fsdp", "tensor"),
        P("fsdp", "tensor"),
        P("tensor", "fsdp"),
        P("tensor"),
        P("tensor"),
        P("tensor"),
    )
    return jax.shard_map(
        run, mesh=mesh, in_specs=in_specs, out_specs=P("fsdp", "tensor"), check_vma=False
    )
```

```python
import math

import jax
import jax.numpy as jnp
from jax import lax
from jax.experimental import pallas as pl
from jax.experimental.pallas import tpu as pltpu
from jax.sharding import PartitionSpec as P

HEAD_DIM = 128
EPS = 1e-06
ROPE_BASE = 500000.0
AXES = ("fsdp", "tensor")


def permute(array, mesh_sizes, target):
    n, tensor_size = mesh_sizes
    pairs = []
    for f in range(n):
        for t in range(tensor_size):
            to_f, to_t = target(f, t)
            pairs.append((f * tensor_size + t, to_f * tensor_size + to_t))
    return lax.ppermute(array, AXES, pairs)


def reverse_bits(value, size):
    result = 0
    while size > 1:
        result = result * 2 + value % 2
        value //= 2
        size //= 2
    return result


def snake(n):
    return list(range(0, n, 2)) + list(range(n - 1, 0, -2))


def gather_tensor(array, sizes):
    have = {0: array}
    bit = sizes[1] // 2
    while bit:
        for r in sorted(have):
            have[r ^ bit] = permute(have[r], sizes, lambda f, t, bit=bit: (f, t ^ bit))
        bit //= 2
    return [have[r] for r in range(sizes[1])]


def ring_gather(top, bottom, sizes):
    n = sizes[0]
    order = snake(n)
    place = {f: i for i, f in enumerate(order)}
    tops, bottoms = [top], [bottom]
    for _ in range(n - 1):
        tops.append(permute(tops[-1], sizes, lambda f, t: (order[(place[f] + 1) % n], t)))
        bottoms.append(permute(bottoms[-1], sizes, lambda f, t: (order[(place[f] - 1) % n], t)))
    return tops, bottoms


def block_product(sizes, sources, choices, tops, bottoms, accumulated, columns, with_squares):
    rows, source_width = sources[0].shape
    half, width = tops[0].shape
    depth = 2 * half
    count = len(tops)
    if depth % 128 or width % 128:
        stack = jnp.stack(sources)
        total = jnp.zeros((rows, columns), jnp.float32) if accumulated is None else accumulated
        for j in range(count):
            piece = lax.dynamic_slice(
                stack, (choices[3 * j], 0, choices[3 * j + 1]), (1, rows, depth)
            )[0]
            matrix = jnp.concatenate([tops[j], bottoms[j]], axis=0)
            term = jnp.dot(piece, matrix, preferred_element_type=jnp.float32)
            current = lax.dynamic_slice(total, (0, choices[3 * j + 2]), (rows, width))
            total = lax.dynamic_update_slice(total, current + term, (0, choices[3 * j + 2]))
        if not with_squares:
            return total
        squares = jnp.sum(total * total, axis=1)
        return total, jnp.broadcast_to(squares[None, :], (8, rows))

    tile = 256 if rows % 256 == 0 else rows
    extra = 0 if accumulated is None else 1
    whole = width == columns

    def kernel(*refs):
        choice = refs[0]
        source = refs[1 : 1 + len(sources)]
        top = refs[1 + len(sources) : 1 + len(sources) + count]
        bottom = refs[1 + len(sources) + count : 1 + len(sources) + 2 * count]
        rest = refs[1 + len(sources) + 2 * count :]
        start = rest[0] if extra else None
        out = rest[extra]
        squares = rest[extra + 1] if with_squares else None
        piece, matrix, sems = rest[-3:]

        def piece_copy(j, which):
            first = pl.multiple_of(choice[3 * j + 1], 128)
            return pltpu.make_async_copy(
                source[which].at[:, pl.ds(first, depth)],
                piece.at[:, pl.ds(j * depth, depth)],
                sems.at[j, 0],
            )

        def matrix_copies(j):
            return (
                pltpu.make_async_copy(top[j], matrix.at[pl.ds(j * depth, half)], sems.at[j, 1]),
                pltpu.make_async_copy(
                    bottom[j], matrix.at[pl.ds(j * depth + half, half)], sems.at[j, 2]
                ),
            )

        for j in range(count):
            for which in range(len(sources)):

                @pl.when(choice[3 * j] == which)
                def _(j=j, which=which):
                    piece_copy(j, which).start()

            for copy in matrix_copies(j):
                copy.start()
        for j in range(count):
            piece_copy(j, 0).wait()
            for copy in matrix_copies(j):
                copy.wait()
        if not whole:
            out[...] = start[...] if extra else jnp.zeros_like(out)
        for lower in range(0, rows, tile):
            part = pl.ds(lower, tile)
            if whole:
                term = jnp.dot(piece[part, :], matrix[...], preferred_element_type=jnp.float32)
                out[part, :] = start[part, :] + term if extra else term
            else:
                for j in range(count):
                    term = jnp.dot(
                        piece[part, pl.ds(j * depth, depth)],
                        matrix[pl.ds(j * depth, depth), :],
                        preferred_element_type=jnp.float32,
                    )
                    span = pl.ds(pl.multiple_of(choice[3 * j + 2], 128), width)
                    out[part, span] += term
            if with_squares:
                total = out[part, :]
                sums = jnp.sum(total * total, axis=1, keepdims=True)
                squares[:, part] = jnp.broadcast_to(sums, (tile, 128)).T[:8]

    any_space = pl.BlockSpec(memory_space=pl.ANY)
    in_vmem = pl.BlockSpec(memory_space=pltpu.VMEM)
    out_shape = [jax.ShapeDtypeStruct((rows, columns), jnp.float32)]
    if with_squares:
        out_shape.append(jax.ShapeDtypeStruct((8, rows), jnp.float32))
    operands = [jnp.stack(choices).astype(jnp.int32), *sources, *tops, *bottoms]
    specs = [pl.BlockSpec(memory_space=pltpu.SMEM)] + [any_space] * (len(operands) - 1)
    if extra:
        operands.append(accumulated)
        specs.append(in_vmem)
    results = pl.pallas_call(
        kernel,
        out_shape=out_shape,
        in_specs=specs,
        out_specs=[in_vmem] * len(out_shape),
        scratch_shapes=[
            pltpu.VMEM((rows, count * depth), sources[0].dtype),
            pltpu.VMEM((count * depth, width), tops[0].dtype),
            pltpu.SemaphoreType.DMA((count, 3)),
        ],
        compiler_params=pltpu.CompilerParams(vmem_limit_bytes=40 * 2**20),
        cost_estimate=pl.CostEstimate(
            flops=2 * rows * count * depth * width,
            bytes_accessed=2 * count * depth * (rows + width) + 8 * rows * columns,
            transcendentals=0,
        ),
    )(*operands)
    return tuple(results) if with_squares else results[0]


def attention(total, sums, cosine, sine, starts, query_gain, key_gain, tensor_size, half_rows):
    capacity = total.shape[0]
    q_width, k_width = query_gain.shape[1], key_gain.shape[1]
    heads, kv_heads = q_width // HEAD_DIM, k_width // HEAD_DIM
    group = heads // kv_heads
    block = 128

    def kernel(*refs):
        total_ref, sum_refs = refs[0], refs[1 : 1 + len(sums)]
        cosine_ref, sine_ref, starts_ref, q_gain_ref, k_gain_ref, out_ref = refs[1 + len(sums) :]
        offset = pl.program_id(0) * half_rows
        squares = sum_refs[0][...]
        for other in sum_refs[1:]:
            squares = squares + other[...]
        q_scale = lax.rsqrt(squares[0:1] / (q_width * tensor_size) + EPS)
        k_scale = lax.rsqrt(squares[1:2] / (k_width * tensor_size) + EPS)
        q_scale = jnp.broadcast_to(q_scale, (HEAD_DIM, half_rows)).T
        k_scale = jnp.broadcast_to(k_scale, (HEAD_DIM, half_rows)).T
        cosines, sines = cosine_ref[...], sine_ref[...]

        def rotated(lower, scale, gain):
            field = total_ref[:, lower : lower + HEAD_DIM] * scale * gain
            return (
                field * cosines + pltpu.roll(field, HEAD_DIM // 2, 1) * sines
            ).astype(jnp.bfloat16)

        for g in range(kv_heads):
            low = g * HEAD_DIM
            keys = rotated(q_width + low, k_scale, k_gain_ref[:, low : low + HEAD_DIM])
            values = total_ref[:, q_width + k_width + low : q_width + k_width + low + HEAD_DIM]
            values = values.astype(jnp.bfloat16)
            queries = []
            for h in range(g * group, (g + 1) * group):
                span = slice(h * HEAD_DIM, (h + 1) * HEAD_DIM)
                queries.append(rotated(h * HEAD_DIM, q_scale, q_gain_ref[:, span]))
            for i in range(half_rows // block):
                lower, reach = i * block, (i + 1) * block
                stacked = jnp.concatenate([q[lower:reach] for q in queries], axis=0)
                scores = lax.dot_general(
                    stacked,
                    keys[:reach],
                    (((1,), (1,)), ((), ())),
                    preferred_element_type=jnp.float32,
                ) * (1.0 / math.sqrt(HEAD_DIM))
                first = starts_ref[lower:reach, :] - offset
                lanes = lax.broadcasted_iota(jnp.int32, (block, block), 1)
                row = lax.broadcasted_iota(jnp.int32, (block, block), 0)
                allowed = jnp.concatenate(
                    [lanes + c * block >= first for c in range(i)]
                    + [(lanes + lower >= first) & (lanes <= row)],
                    axis=1,
                )
                scores = scores.reshape(group, block, reach)
                scores = jnp.where(allowed[None], scores, jnp.float32(-1e30))
                peak = jnp.max(scores, axis=-1, keepdims=True)
                expo = jnp.exp(scores - peak)
                probs = expo / jnp.sum(expo, axis=-1, keepdims=True)
                probs = probs.astype(jnp.bfloat16).reshape(group * block, reach)
                mixed = jnp.dot(probs, values[:reach], preferred_element_type=jnp.float32)
                mixed = mixed.astype(jnp.bfloat16)
                for h in range(group):
                    column = (g * group + h) * HEAD_DIM
                    out_ref[lower:reach, column : column + HEAD_DIM] = mixed[
                        h * block : (h + 1) * block
                    ]

    def by_rows(width):
        return pl.BlockSpec((half_rows, width), lambda i: (i, 0))

    def constant(width):
        return pl.BlockSpec((1, width), lambda i: (0, 0))

    return pl.pallas_call(
        kernel,
        grid=(capacity // half_rows,),
        out_shape=jax.ShapeDtypeStruct((capacity, q_width), jnp.bfloat16),
        in_specs=[by_rows(total.shape[1])]
        + [pl.BlockSpec((8, half_rows), lambda i: (0, i))] * len(sums)
        + [by_rows(HEAD_DIM)] * 3
        + [constant(q_width), constant(k_width)],
        out_specs=by_rows(q_width),
        compiler_params=pltpu.CompilerParams(vmem_limit_bytes=40 * 2**20),
        cost_estimate=pl.CostEstimate(
            flops=4 * capacity * half_rows * q_width,
            bytes_accessed=8 * capacity * total.shape[1],
            transcendentals=capacity * half_rows * heads,
        ),
    )(total, *sums, cosine, sine, starts, query_gain, key_gain)


def finish(attn_out, sums, tokens, out_gain, live_rows, features):
    rows, width = tokens.shape
    tile = 256 if rows % 256 == 0 else rows

    def kernel(*refs):
        live_ref, attn_ref, sum_refs = refs[0], refs[1], refs[2 : 2 + len(sums)]
        tokens_ref, gain_ref, out_ref = refs[2 + len(sums) :]
        squares = sum_refs[0][...]
        for other in sum_refs[1:]:
            squares = squares + other[...]
        scale = lax.rsqrt(squares[0:1] / features + EPS)
        scale = jnp.broadcast_to(scale, (128, tile)).T
        row = pl.program_id(0) * tile + lax.broadcasted_iota(jnp.int32, (tile, 128), 0)
        live = row < live_ref[0]
        for lower in range(0, width, 128):
            span = slice(lower, lower + 128)
            value = tokens_ref[:, span].astype(jnp.float32) + attn_ref[:, span] * scale * gain_ref[:, span]
            out_ref[:, span] = jnp.where(live, value, 0.0).astype(jnp.bfloat16)

    return pl.pallas_call(
        kernel,
        grid=(rows // tile,),
        out_shape=jax.ShapeDtypeStruct((rows, width), jnp.bfloat16),
        in_specs=[
            pl.BlockSpec(memory_space=pltpu.SMEM),
            pl.BlockSpec((tile, width), lambda i: (i, 0)),
        ]
        + [pl.BlockSpec((8, tile), lambda i: (0, i))] * len(sums)
        + [
            pl.BlockSpec((tile, width), lambda i: (i, 0)),
            pl.BlockSpec((1, width), lambda i: (0, 0)),
        ],
        out_specs=pl.BlockSpec((tile, width), lambda i: (i, 0)),
        compiler_params=pltpu.CompilerParams(vmem_limit_bytes=32 * 2**20),
    )(live_rows, attn_out, *sums, tokens, out_gain)


def body(
    sizes, tokens, live_rows, first_row, w_query, w_key, w_value, w_out, query_gain, key_gain, out_gain
):
    n, tensor_size = sizes
    capacity, width = tokens.shape
    half_rows = capacity // 2
    per_tensor = n // tensor_size
    f_index = lax.axis_index("fsdp")
    t_index = lax.axis_index("tensor")
    order = snake(n)
    place = [order.index(f) for f in range(n)]
    order_of = jnp.array(order, jnp.int32)
    position = jnp.array(place, jnp.int32)[f_index]

    weights = jnp.concatenate([w_query, w_key, w_value], axis=1)
    depth = weights.shape[0]
    half = depth // 2
    token_blocks = gather_tensor(tokens, sizes)
    tops, bottoms = ring_gather(weights[:half], weights[half:], sizes)

    moved = permute(
        w_out,
        sizes,
        lambda f, t: (
            ((f // per_tensor) ^ reverse_bits(t, tensor_size)) * per_tensor + f % per_tensor,
            t,
        ),
    )
    moved = permute(
        moved, sizes, lambda f, t: (f, (f // per_tensor) ^ reverse_bits(t, tensor_size))
    )

    q_width, k_width = w_query.shape[1], w_key.shape[1]
    columns = weights.shape[1]
    steps = [[0, n // 2]] + [[s, n - s] for s in range(n // 2 + 1, n)]
    early = [offset for group in steps[: len(steps) // 2] for offset in group]
    late = [offset for group in steps[len(steps) // 2 :] for offset in group]

    def source_blocks(offsets):
        return [order_of[lax.rem(position + offset, n)] for offset in offsets]

    total = None
    for offsets in (early, late):
        choices = []
        for block in source_blocks(offsets):
            choices += [
                (block // per_tensor) ^ t_index,
                lax.rem(block, per_tensor) * depth,
                jnp.int32(0),
            ]
        total = block_product(
            sizes,
            token_blocks,
            choices,
            [tops[(n - offset) % n] for offset in offsets],
            [bottoms[offset] for offset in offsets],
            total,
            columns,
            False,
        )

    out_half = w_out.shape[0] // 2
    out_top, out_bottom, _ = lax.optimization_barrier(
        (moved[:out_half], moved[out_half:], (tops[-1], bottoms[-1]))
    )
    out_tops, out_bottoms = ring_gather(out_top, out_bottom, sizes)

    query = total[:, :q_width]
    key = total[:, q_width : q_width + k_width]
    squares = jnp.stack([jnp.sum(query * query, axis=1), jnp.sum(key * key, axis=1)])
    squares = jnp.concatenate([squares, jnp.zeros((6, capacity), jnp.float32)])
    square_blocks = gather_tensor(squares, sizes)
    row_ids = jnp.arange(capacity, dtype=jnp.int32)
    positions = (row_ids - first_row).astype(jnp.float32)
    half_dim = HEAD_DIM // 2
    freqs = jnp.power(
        ROPE_BASE, -(jnp.arange(half_dim, dtype=jnp.float32) * 2.0 / HEAD_DIM)
    )
    angle = positions[:, None] * freqs[None, :]
    cosine, sine = jnp.cos(angle), jnp.sin(angle)
    attended = attention(
        total,
        square_blocks,
        jnp.concatenate([cosine, cosine], axis=1),
        jnp.concatenate([-sine, sine], axis=1),
        jnp.broadcast_to(first_row[:, None], (capacity, HEAD_DIM)),
        query_gain[None, :],
        key_gain[None, :],
        tensor_size,
        half_rows,
    )
    attended_blocks = gather_tensor(attended, sizes)

    reversed_of = jnp.array(
        [reverse_bits(t, tensor_size) for t in range(tensor_size)], jnp.int32
    )
    attn_out = None
    for offsets in (early, late):
        choices = []
        for block in source_blocks(offsets):
            choices += [
                reversed_of[(block // per_tensor) ^ t_index] ^ t_index,
                jnp.int32(0),
                lax.rem(block, per_tensor) * w_out.shape[1],
            ]
        attn_out = block_product(
            sizes,
            attended_blocks,
            choices,
            [out_tops[(n - offset) % n] for offset in offsets],
            [out_bottoms[offset] for offset in offsets],
            attn_out,
            width,
            offsets is late,
        )
    attn_out, out_squares = attn_out
    return finish(
        attn_out,
        gather_tensor(out_squares, sizes),
        tokens,
        out_gain[None, :],
        live_rows,
        width * tensor_size,
    )


def solution(mesh):
    sizes = (mesh.shape["fsdp"], mesh.shape["tensor"])

    def run(*arrays):
        return body(sizes, *arrays)

    in_specs = (
        P("fsdp", "tensor"),
        P("fsdp"),
        P("fsdp"),
        P("fsdp", "tensor"),
        P("fsdp", "tensor"),
        P("fsdp", "tensor"),
        P("tensor", "fsdp"),
        P("tensor"),
        P("tensor"),
        P("tensor"),
    )
    return jax.shard_map(
        run, mesh=mesh, in_specs=in_specs, out_specs=P("fsdp", "tensor"), check_vma=False
    )
```

```python
import math

import jax
import jax.numpy as jnp
from jax import lax
from jax.experimental import pallas as pl
from jax.experimental.pallas import tpu as pltpu
from jax.sharding import PartitionSpec as P

HEAD_DIM = 128
EPS = 1e-06
ROPE_BASE = 500000.0
AXES = ("fsdp", "tensor")


def permute(array, mesh_sizes, target):
    n, tensor_size = mesh_sizes
    pairs = []
    for f in range(n):
        for t in range(tensor_size):
            to_f, to_t = target(f, t)
            pairs.append((f * tensor_size + t, to_f * tensor_size + to_t))
    return lax.ppermute(array, AXES, pairs)


def reverse_bits(value, size):
    result = 0
    while size > 1:
        result = result * 2 + value % 2
        value //= 2
        size //= 2
    return result


def snake(n):
    return list(range(0, n, 2)) + list(range(n - 1, 0, -2))


def gather_tensor(array, sizes):
    have = {0: array}
    bit = sizes[1] // 2
    while bit:
        for r in sorted(have):
            have[r ^ bit] = permute(have[r], sizes, lambda f, t, bit=bit: (f, t ^ bit))
        bit //= 2
    return [have[r] for r in range(sizes[1])]


def ring_gather(top, bottom, sizes):
    n = sizes[0]
    order = snake(n)
    place = {f: i for i, f in enumerate(order)}
    tops, bottoms = [top], [bottom]
    for _ in range(n - 1):
        tops.append(permute(tops[-1], sizes, lambda f, t: (order[(place[f] + 1) % n], t)))
        bottoms.append(permute(bottoms[-1], sizes, lambda f, t: (order[(place[f] - 1) % n], t)))
    return tops, bottoms


def snake_block(sizes, f_index, offset):
    n = sizes[0]
    ahead = lax.rem(f_index, 2) == 0
    position = jnp.where(ahead, f_index // 2, n - 1 - f_index // 2)
    place = lax.rem(position + offset, n)
    return jnp.where(place < (n + 1) // 2, 2 * place, 2 * (n - place) - 1)


def traced_reverse(value, size):
    result = value * 0
    while size > 1:
        result = result * 2 + lax.rem(value, 2)
        value = value // 2
        size //= 2
    return result


def block_product(sizes, sources, choose, offsets, tops, bottoms, accumulated, columns, spans):
    rows, source_width = sources[0].shape
    tops = [tops[(sizes[0] - offset) % sizes[0]] for offset in offsets]
    bottoms = [bottoms[offset] for offset in offsets]
    half, width = tops[0].shape
    depth = 2 * half
    count = len(tops)
    if depth % 128 or width % 128:
        stack = jnp.stack(sources)
        total = jnp.zeros((rows, columns), jnp.float32) if accumulated is None else accumulated
        for j in range(count):
            which, first, column = choose(offsets[j])
            piece = lax.dynamic_slice(stack, (which, 0, first), (1, rows, depth))[0]
            matrix = jnp.concatenate([tops[j], bottoms[j]], axis=0)
            term = jnp.dot(piece, matrix, preferred_element_type=jnp.float32)
            current = lax.dynamic_slice(total, (0, column), (rows, width))
            total = lax.dynamic_update_slice(total, current + term, (0, column))
        if spans is None:
            return total
        squares = [jnp.sum(total[:, low:high] ** 2, axis=1) for low, high in spans]
        squares += [jnp.zeros_like(squares[0])] * (8 - len(squares))
        return total, jnp.stack(squares)

    tile = 256 if rows % 256 == 0 else rows
    tiles = rows // tile
    extra = 0 if accumulated is None else 1
    whole = width == columns

    def kernel(*refs):
        source, refs = refs[: len(sources)], refs[len(sources) :]
        top, refs = refs[:count], refs[count:]
        bottom, refs = refs[:count], refs[count:]
        start, refs = refs[:extra], refs[extra:]
        out, refs = refs[0], refs[1:]
        squares, refs = refs[: spans is not None], refs[spans is not None :]
        piece, matrix, total, sems, tile_sems = refs
        choices = [choose(offset) for offset in offsets]

        def piece_copy(j, which):
            first = choices[j][1]
            if not isinstance(first, int):
                first = pl.multiple_of(first, 128)
            return pltpu.make_async_copy(
                source[which].at[:, pl.ds(first, depth)],
                piece.at[:, pl.ds(j * depth, depth)],
                sems.at[j, 0],
            )

        def matrix_copies(j):
            return (
                pltpu.make_async_copy(top[j], matrix.at[pl.ds(j * depth, half)], sems.at[j, 1]),
                pltpu.make_async_copy(
                    bottom[j], matrix.at[pl.ds(j * depth + half, half)], sems.at[j, 2]
                ),
            )

        def in_copy(i):
            part = pl.ds(i * tile, tile)
            return pltpu.make_async_copy(start[0].at[part], total.at[part], tile_sems.at[i, 0])

        def out_copy(i):
            part = pl.ds(i * tile, tile)
            return pltpu.make_async_copy(total.at[part], out.at[part], tile_sems.at[i, 1])

        for j in range(count):
            for which in range(len(sources)):

                @pl.when(choices[j][0] == which)
                def _(j=j, which=which):
                    piece_copy(j, which).start()

            for copy in matrix_copies(j):
                copy.start()
        for i in range(tiles * extra):
            in_copy(i).start()
        for j in range(count):
            piece_copy(j, 0).wait()
            for copy in matrix_copies(j):
                copy.wait()
        for i in range(tiles):
            part = pl.ds(i * tile, tile)
            if extra:
                in_copy(i).wait()
            if whole:
                term = jnp.dot(piece[part, :], matrix[...], preferred_element_type=jnp.float32)
                total[part, :] = total[part, :] + term if extra else term
            else:
                if not extra:
                    total[part, :] = jnp.zeros((tile, columns), jnp.float32)
                for j in range(count):
                    term = jnp.dot(
                        piece[part, pl.ds(j * depth, depth)],
                        matrix[pl.ds(j * depth, depth), :],
                        preferred_element_type=jnp.float32,
                    )
                    total[part, pl.ds(pl.multiple_of(choices[j][2], 128), width)] += term
            out_copy(i).start()
            if spans is not None:
                sums = []
                for low, high in spans:
                    chosen = total[part, low:high]
                    chosen = jnp.sum(chosen * chosen, axis=1, keepdims=True)
                    sums.append(jnp.broadcast_to(chosen, (tile, 128)).T[:8])
                lines = lax.broadcasted_iota(jnp.int32, (8, tile), 0)
                line = sums[0]
                for index in range(1, len(sums)):
                    line = jnp.where(lines == index, sums[index], line)
                squares[0][:, part] = line
        for i in range(tiles):
            out_copy(i).wait()

    any_space = pl.BlockSpec(memory_space=pl.ANY)
    out_shape = [jax.ShapeDtypeStruct((rows, columns), jnp.float32)]
    out_specs = [any_space]
    if spans is not None:
        out_shape.append(jax.ShapeDtypeStruct((8, rows), jnp.float32))
        out_specs.append(pl.BlockSpec(memory_space=pltpu.VMEM))
    operands = [*sources, *tops, *bottoms] + [accumulated] * extra
    needed = 2 * count * depth * (rows + width) + 4 * rows * columns
    results = pl.pallas_call(
        kernel,
        out_shape=out_shape,
        in_specs=[any_space] * len(operands),
        out_specs=out_specs,
        scratch_shapes=[
            pltpu.VMEM((rows, count * depth), sources[0].dtype),
            pltpu.VMEM((count * depth, width), tops[0].dtype),
            pltpu.VMEM((rows, columns), jnp.float32),
            pltpu.SemaphoreType.DMA((count, 3)),
            pltpu.SemaphoreType.DMA((tiles, 2)),
        ],
        compiler_params=pltpu.CompilerParams(vmem_limit_bytes=needed + 6 * 2**20),
        cost_estimate=pl.CostEstimate(
            flops=2 * rows * count * depth * width,
            bytes_accessed=2 * count * depth * (rows + width) + 8 * rows * columns,
            transcendentals=0,
        ),
    )(*operands)
    return tuple(results) if spans is not None else results[0]


def attention(total, sums, cosine, sine, starts, query_gain, key_gain, tensor_size, half_rows):
    capacity = total.shape[0]
    q_width, k_width = query_gain.shape[1], key_gain.shape[1]
    heads, kv_heads = q_width // HEAD_DIM, k_width // HEAD_DIM
    group = heads // kv_heads
    block = 128

    def kernel(*refs):
        total_ref, sum_refs = refs[0], refs[1 : 1 + len(sums)]
        cosine_ref, sine_ref, starts_ref, q_gain_ref, k_gain_ref, out_ref = refs[1 + len(sums) :]
        offset = pl.program_id(0) * half_rows
        squares = sum_refs[0][...]
        for other in sum_refs[1:]:
            squares = squares + other[...]
        q_scale = lax.rsqrt(squares[0:1] / (q_width * tensor_size) + EPS)
        k_scale = lax.rsqrt(squares[1:2] / (k_width * tensor_size) + EPS)
        q_scale = jnp.broadcast_to(q_scale, (HEAD_DIM, half_rows)).T
        k_scale = jnp.broadcast_to(k_scale, (HEAD_DIM, half_rows)).T
        cosines, sines = cosine_ref[...], sine_ref[...]

        def rotated(lower, scale, gain):
            field = total_ref[:, lower : lower + HEAD_DIM] * scale * gain
            return (
                field * cosines + pltpu.roll(field, HEAD_DIM // 2, 1) * sines
            ).astype(jnp.bfloat16)

        for g in range(kv_heads):
            low = g * HEAD_DIM
            keys = rotated(q_width + low, k_scale, k_gain_ref[:, low : low + HEAD_DIM])
            values = total_ref[:, q_width + k_width + low : q_width + k_width + low + HEAD_DIM]
            values = values.astype(jnp.bfloat16)
            queries = []
            for h in range(g * group, (g + 1) * group):
                span = slice(h * HEAD_DIM, (h + 1) * HEAD_DIM)
                queries.append(rotated(h * HEAD_DIM, q_scale, q_gain_ref[:, span]))
            for i in range(half_rows // block):
                lower, reach = i * block, (i + 1) * block
                stacked = jnp.concatenate([q[lower:reach] for q in queries], axis=0)
                scores = lax.dot_general(
                    stacked,
                    keys[:reach],
                    (((1,), (1,)), ((), ())),
                    preferred_element_type=jnp.float32,
                ) * (1.0 / math.sqrt(HEAD_DIM))
                first = starts_ref[lower:reach, :] - offset
                lanes = lax.broadcasted_iota(jnp.int32, (block, block), 1)
                row = lax.broadcasted_iota(jnp.int32, (block, block), 0)
                allowed = jnp.concatenate(
                    [lanes + c * block >= first for c in range(i)]
                    + [(lanes + lower >= first) & (lanes <= row)],
                    axis=1,
                )
                scores = scores.reshape(group, block, reach)
                scores = jnp.where(allowed[None], scores, jnp.float32(-1e30))
                peak = jnp.max(scores, axis=-1, keepdims=True)
                expo = jnp.exp(scores - peak)
                probs = expo / jnp.sum(expo, axis=-1, keepdims=True)
                probs = probs.astype(jnp.bfloat16).reshape(group * block, reach)
                mixed = jnp.dot(probs, values[:reach], preferred_element_type=jnp.float32)
                mixed = mixed.astype(jnp.bfloat16)
                for h in range(group):
                    column = (g * group + h) * HEAD_DIM
                    out_ref[lower:reach, column : column + HEAD_DIM] = mixed[
                        h * block : (h + 1) * block
                    ]

    def by_rows(width):
        return pl.BlockSpec((half_rows, width), lambda i: (i, 0))

    def constant(width):
        return pl.BlockSpec((1, width), lambda i: (0, 0))

    return pl.pallas_call(
        kernel,
        grid=(capacity // half_rows,),
        out_shape=jax.ShapeDtypeStruct((capacity, q_width), jnp.bfloat16),
        in_specs=[by_rows(total.shape[1])]
        + [pl.BlockSpec((8, half_rows), lambda i: (0, i))] * len(sums)
        + [by_rows(HEAD_DIM)] * 3
        + [constant(q_width), constant(k_width)],
        out_specs=by_rows(q_width),
        compiler_params=pltpu.CompilerParams(vmem_limit_bytes=24 * 2**20),
        cost_estimate=pl.CostEstimate(
            flops=4 * capacity * half_rows * q_width,
            bytes_accessed=8 * capacity * total.shape[1],
            transcendentals=capacity * half_rows * heads,
        ),
    )(total, *sums, cosine, sine, starts, query_gain, key_gain)


def finish(attn_out, sums, tokens, out_gain, live_rows, features):
    rows, width = tokens.shape
    tile = 256 if rows % 256 == 0 else rows

    def kernel(*refs):
        live_ref, attn_ref, sum_refs = refs[0], refs[1], refs[2 : 2 + len(sums)]
        tokens_ref, gain_ref, out_ref = refs[2 + len(sums) :]
        squares = sum_refs[0][...]
        for other in sum_refs[1:]:
            squares = squares + other[...]
        scale = lax.rsqrt(squares[0:1] / features + EPS)
        scale = jnp.broadcast_to(scale, (128, tile)).T
        row = pl.program_id(0) * tile + lax.broadcasted_iota(jnp.int32, (tile, 128), 0)
        live = row < live_ref[0]
        for lower in range(0, width, 128):
            span = slice(lower, lower + 128)
            value = tokens_ref[:, span].astype(jnp.float32) + attn_ref[:, span] * scale * gain_ref[:, span]
            out_ref[:, span] = jnp.where(live, value, 0.0).astype(jnp.bfloat16)

    return pl.pallas_call(
        kernel,
        grid=(rows // tile,),
        out_shape=jax.ShapeDtypeStruct((rows, width), jnp.bfloat16),
        in_specs=[
            pl.BlockSpec(memory_space=pltpu.SMEM),
            pl.BlockSpec((tile, width), lambda i: (i, 0)),
        ]
        + [pl.BlockSpec((8, tile), lambda i: (0, i))] * len(sums)
        + [
            pl.BlockSpec((tile, width), lambda i: (i, 0)),
            pl.BlockSpec((1, width), lambda i: (0, 0)),
        ],
        out_specs=pl.BlockSpec((tile, width), lambda i: (i, 0)),
        compiler_params=pltpu.CompilerParams(vmem_limit_bytes=16 * 2**20),
    )(live_rows, attn_out, *sums, tokens, out_gain)


def body(
    sizes, tokens, live_rows, first_row, w_query, w_key, w_value, w_out, query_gain, key_gain, out_gain
):
    n, tensor_size = sizes
    capacity, width = tokens.shape
    half_rows = capacity // 2
    per_tensor = n // tensor_size

    weights = jnp.concatenate([w_query, w_key, w_value], axis=1)
    depth = weights.shape[0]
    half = depth // 2
    token_blocks = gather_tensor(tokens, sizes)
    tops, bottoms = ring_gather(weights[:half], weights[half:], sizes)

    moved = permute(
        w_out,
        sizes,
        lambda f, t: (
            ((f // per_tensor) ^ reverse_bits(t, tensor_size)) * per_tensor + f % per_tensor,
            t,
        ),
    )
    moved = permute(
        moved, sizes, lambda f, t: (f, (f // per_tensor) ^ reverse_bits(t, tensor_size))
    )

    q_width, k_width = w_query.shape[1], w_key.shape[1]
    columns = weights.shape[1]
    steps = [[0, n // 2]] + [[s, n - s] for s in range(n // 2 + 1, n)]
    middle = (len(steps) + 1) // 2
    groups = [[offset for group in steps[:middle] for offset in group]] + steps[middle:]

    def choose_tokens(offset):
        block = snake_block(sizes, lax.axis_index("fsdp"), offset)
        which = (block // per_tensor) ^ lax.axis_index("tensor")
        return which, lax.rem(block, per_tensor) * depth, 0

    total = None
    for number, offsets in enumerate(groups):
        total = block_product(
            sizes,
            token_blocks,
            choose_tokens,
            offsets,
            tops,
            bottoms,
            total,
            columns,
            [(0, q_width), (q_width, q_width + k_width)] if number == len(groups) - 1 else None,
        )
    total, squares = total

    out_half = w_out.shape[0] // 2
    out_top, out_bottom, _ = lax.optimization_barrier(
        (moved[:out_half], moved[out_half:], (tops[-1], bottoms[-1]))
    )
    out_tops, out_bottoms = ring_gather(out_top, out_bottom, sizes)

    square_blocks = gather_tensor(squares, sizes)
    row_ids = jnp.arange(capacity, dtype=jnp.int32)
    positions = (row_ids - first_row).astype(jnp.float32)
    half_dim = HEAD_DIM // 2
    freqs = jnp.power(
        ROPE_BASE, -(jnp.arange(half_dim, dtype=jnp.float32) * 2.0 / HEAD_DIM)
    )
    angle = positions[:, None] * freqs[None, :]
    cosine, sine = jnp.cos(angle), jnp.sin(angle)
    attended = attention(
        total,
        square_blocks,
        jnp.concatenate([cosine, cosine], axis=1),
        jnp.concatenate([-sine, sine], axis=1),
        jnp.broadcast_to(first_row[:, None], (capacity, HEAD_DIM)),
        query_gain[None, :],
        key_gain[None, :],
        tensor_size,
        half_rows,
    )
    attended_blocks = gather_tensor(attended, sizes)

    def choose_attended(offset):
        block = snake_block(sizes, lax.axis_index("fsdp"), offset)
        t_index = lax.axis_index("tensor")
        source = traced_reverse((block // per_tensor) ^ t_index, tensor_size)
        return source ^ t_index, 0, lax.rem(block, per_tensor) * w_out.shape[1]

    attn_out = None
    for number, offsets in enumerate(groups):
        attn_out = block_product(
            sizes,
            attended_blocks,
            choose_attended,
            offsets,
            out_tops,
            out_bottoms,
            attn_out,
            width,
            [(0, width)] if number == len(groups) - 1 else None,
        )
    attn_out, out_squares = attn_out
    return finish(
        attn_out,
        gather_tensor(out_squares, sizes),
        tokens,
        out_gain[None, :],
        live_rows,
        width * tensor_size,
    )


def solution(mesh):
    sizes = (mesh.shape["fsdp"], mesh.shape["tensor"])

    def run(*arrays):
        return body(sizes, *arrays)

    in_specs = (
        P("fsdp", "tensor"),
        P("fsdp"),
        P("fsdp"),
        P("fsdp", "tensor"),
        P("fsdp", "tensor"),
        P("fsdp", "tensor"),
        P("tensor", "fsdp"),
        P("tensor"),
        P("tensor"),
        P("tensor"),
    )
    return jax.shard_map(
        run, mesh=mesh, in_specs=in_specs, out_specs=P("fsdp", "tensor"), check_vma=False
    )
```

```python
import math

import jax
import jax.numpy as jnp
from jax import lax
from jax.experimental import pallas as pl
from jax.experimental.pallas import tpu as pltpu
from jax.sharding import PartitionSpec as P

HEAD_DIM = 128
EPS = 1e-06
ROPE_BASE = 500000.0
AXES = ("fsdp", "tensor")


def permute(array, mesh_sizes, target):
    n, tensor_size = mesh_sizes
    pairs = []
    for f in range(n):
        for t in range(tensor_size):
            to_f, to_t = target(f, t)
            pairs.append((f * tensor_size + t, to_f * tensor_size + to_t))
    return lax.ppermute(array, AXES, pairs)


def reverse_bits(value, size):
    result = 0
    while size > 1:
        result = result * 2 + value % 2
        value //= 2
        size //= 2
    return result


def snake(n):
    return list(range(0, n, 2)) + list(range(n - 1, 0, -2))


def gather_tensor(array, sizes):
    have = {0: array}
    bit = sizes[1] // 2
    while bit:
        for r in sorted(have):
            have[r ^ bit] = permute(have[r], sizes, lambda f, t, bit=bit: (f, t ^ bit))
        bit //= 2
    return [have[r] for r in range(sizes[1])]


def swap_small(array, sizes):
    return [array] + [
        permute(array, sizes, lambda f, t, r=r: (f, t ^ r)) for r in range(1, sizes[1])
    ]


def pack_weights(parts):
    rows = parts[0].shape[0]
    half = rows // 2
    widths = [part.shape[1] for part in parts]
    if any(width % 128 for width in widths) or half % 16:
        packed = jnp.concatenate(parts, axis=1)
        return packed[:half], packed[half:]

    def kernel(*refs):
        sources, outs, sems = refs[: len(parts)], refs[len(parts) : -1], refs[-1]
        copies = []
        first = 0
        for number, (source, width) in enumerate(zip(sources, widths)):
            for side in range(2):
                copies.append(
                    pltpu.make_async_copy(
                        source.at[pl.ds(side * half, half)],
                        outs[side].at[:, pl.ds(first, width)],
                        sems.at[number, side],
                    )
                )
            first += width
        for copy in copies:
            copy.start()
        for copy in copies:
            copy.wait()

    shape = jax.ShapeDtypeStruct((half, sum(widths)), parts[0].dtype)
    any_space = pl.BlockSpec(memory_space=pl.ANY)
    return pl.pallas_call(
        kernel,
        out_shape=[shape, shape],
        in_specs=[any_space] * len(parts),
        out_specs=[any_space] * 2,
        scratch_shapes=[pltpu.SemaphoreType.DMA((len(parts), 2))],
    )(*parts)


def ring_gather(top, bottom, sizes, ties):
    n = sizes[0]
    order = snake(n)
    place = {f: i for i, f in enumerate(order)}
    tops, bottoms = [top], [bottom]
    for step in range(1, n):
        tops.append(permute(tops[-1], sizes, lambda f, t: (order[(place[f] + 1) % n], t)))
        bottoms.append(permute(bottoms[-1], sizes, lambda f, t: (order[(place[f] - 1) % n], t)))
        if step in ties:
            tied = ties[step](tops, bottoms)
            tops[-1], bottoms[-1], ties[step] = lax.optimization_barrier(
                (tops[-1], bottoms[-1], tied)
            )
    return tops, bottoms


def snake_block(sizes, f_index, offset):
    n = sizes[0]
    ahead = lax.rem(f_index, 2) == 0
    position = jnp.where(ahead, f_index // 2, n - 1 - f_index // 2)
    place = lax.rem(position + offset, n)
    return jnp.where(place < (n + 1) // 2, 2 * place, 2 * (n - place) - 1)


def traced_reverse(value, size):
    result = value * 0
    while size > 1:
        result = result * 2 + lax.rem(value, 2)
        value = value // 2
        size //= 2
    return result


def block_product(sizes, sources, choose, offsets, tops, bottoms, accumulated, columns, spans):
    rows, source_width = sources[0].shape
    tops = [tops[(sizes[0] - offset) % sizes[0]] for offset in offsets]
    bottoms = [bottoms[offset] for offset in offsets]
    half, width = tops[0].shape
    depth = 2 * half
    count = len(tops)
    if depth % 128 or width % 128:
        stack = jnp.stack(sources)
        total = jnp.zeros((rows, columns), jnp.float32) if accumulated is None else accumulated
        for j in range(count):
            which, first, column = choose(offsets[j])
            piece = lax.dynamic_slice(stack, (which, 0, first), (1, rows, depth))[0]
            matrix = jnp.concatenate([tops[j], bottoms[j]], axis=0)
            term = jnp.dot(piece, matrix, preferred_element_type=jnp.float32)
            current = lax.dynamic_slice(total, (0, column), (rows, width))
            total = lax.dynamic_update_slice(total, current + term, (0, column))
        if spans is None:
            return total
        squares = [jnp.sum(total[:, low:high] ** 2, axis=1) for low, high in spans]
        squares += [jnp.zeros_like(squares[0])] * (8 - len(squares))
        return total, jnp.stack(squares)

    tile = 256 if rows % 256 == 0 else rows
    tiles = rows // tile
    extra = 0 if accumulated is None else 1
    whole = width == columns

    def kernel(*refs):
        source, refs = refs[: len(sources)], refs[len(sources) :]
        top, refs = refs[:count], refs[count:]
        bottom, refs = refs[:count], refs[count:]
        start, refs = refs[:extra], refs[extra:]
        out, refs = refs[0], refs[1:]
        squares, refs = refs[: spans is not None], refs[spans is not None :]
        piece, matrix, total, sems, tile_sems = refs
        choices = [choose(offset) for offset in offsets]

        def piece_copy(j, which):
            first = choices[j][1]
            if not isinstance(first, int):
                first = pl.multiple_of(first, 128)
            return pltpu.make_async_copy(
                source[which].at[:, pl.ds(first, depth)],
                piece.at[:, pl.ds(j * depth, depth)],
                sems.at[j, 0],
            )

        def matrix_copies(j):
            return (
                pltpu.make_async_copy(top[j], matrix.at[pl.ds(j * depth, half)], sems.at[j, 1]),
                pltpu.make_async_copy(
                    bottom[j], matrix.at[pl.ds(j * depth + half, half)], sems.at[j, 2]
                ),
            )

        def in_copy(i):
            part = pl.ds(i * tile, tile)
            return pltpu.make_async_copy(start[0].at[part], total.at[part], tile_sems.at[i, 0])

        def out_copy(i):
            part = pl.ds(i * tile, tile)
            return pltpu.make_async_copy(total.at[part], out.at[part], tile_sems.at[i, 1])

        for j in range(count):
            for which in range(len(sources)):

                @pl.when(choices[j][0] == which)
                def _(j=j, which=which):
                    piece_copy(j, which).start()

            for copy in matrix_copies(j):
                copy.start()
        for i in range(tiles * extra):
            in_copy(i).start()
        together = 2 if whole else 1
        for low in range(0, count, together):
            blocks = range(low, min(low + together, count))
            for j in blocks:
                piece_copy(j, 0).wait()
                for copy in matrix_copies(j):
                    copy.wait()
            span = pl.ds(low * depth, len(blocks) * depth)
            for i in range(tiles):
                part = pl.ds(i * tile, tile)
                if low == 0 and extra:
                    in_copy(i).wait()
                if low == 0 and not extra and not whole:
                    total[part, :] = jnp.zeros((tile, columns), jnp.float32)
                term = jnp.dot(piece[part, span], matrix[span, :], preferred_element_type=jnp.float32)
                if whole:
                    total[part, :] = total[part, :] + term if extra or low else term
                else:
                    total[part, pl.ds(pl.multiple_of(choices[low][2], 128), width)] += term
                if blocks[-1] < count - 1:
                    continue
                out_copy(i).start()
                if spans is not None:
                    sums = []
                    for first, last in spans:
                        chosen = total[part, first:last]
                        chosen = jnp.sum(chosen * chosen, axis=1, keepdims=True)
                        sums.append(jnp.broadcast_to(chosen, (tile, 128)).T[:8])
                    lines = lax.broadcasted_iota(jnp.int32, (8, tile), 0)
                    line = sums[0]
                    for index in range(1, len(sums)):
                        line = jnp.where(lines == index, sums[index], line)
                    squares[0][:, part] = line
        for i in range(tiles):
            out_copy(i).wait()

    any_space = pl.BlockSpec(memory_space=pl.ANY)
    out_shape = [jax.ShapeDtypeStruct((rows, columns), jnp.float32)]
    out_specs = [any_space]
    if spans is not None:
        out_shape.append(jax.ShapeDtypeStruct((8, rows), jnp.float32))
        out_specs.append(pl.BlockSpec(memory_space=pltpu.VMEM))
    operands = [*sources, *tops, *bottoms] + [accumulated] * extra
    needed = 2 * count * depth * (rows + width) + 4 * rows * columns
    results = pl.pallas_call(
        kernel,
        out_shape=out_shape,
        in_specs=[any_space] * len(operands),
        out_specs=out_specs,
        scratch_shapes=[
            pltpu.VMEM((rows, count * depth), sources[0].dtype),
            pltpu.VMEM((count * depth, width), tops[0].dtype),
            pltpu.VMEM((rows, columns), jnp.float32),
            pltpu.SemaphoreType.DMA((count, 3)),
            pltpu.SemaphoreType.DMA((tiles, 2)),
        ],
        compiler_params=pltpu.CompilerParams(vmem_limit_bytes=needed + 6 * 2**20),
        cost_estimate=pl.CostEstimate(
            flops=2 * rows * count * depth * width,
            bytes_accessed=2 * count * depth * (rows + width) + 8 * rows * columns,
            transcendentals=0,
        ),
    )(*operands)
    return tuple(results) if spans is not None else results[0]


def attention(total, sums, cosine, sine, starts, query_gain, key_gain, tensor_size, half_rows):
    capacity = total.shape[0]
    q_width, k_width = query_gain.shape[1], key_gain.shape[1]
    heads, kv_heads = q_width // HEAD_DIM, k_width // HEAD_DIM
    group = heads // kv_heads
    block = 128

    def kernel(*refs):
        total_ref, sum_refs = refs[0], refs[1 : 1 + len(sums)]
        cosine_ref, sine_ref, starts_ref, q_gain_ref, k_gain_ref, out_ref = refs[1 + len(sums) :]
        offset = pl.program_id(0) * half_rows
        squares = sum_refs[0][...]
        for other in sum_refs[1:]:
            squares = squares + other[...]
        q_scale = lax.rsqrt(squares[0:1] / (q_width * tensor_size) + EPS)
        k_scale = lax.rsqrt(squares[1:2] / (k_width * tensor_size) + EPS)
        q_scale = jnp.broadcast_to(q_scale, (HEAD_DIM, half_rows)).T
        k_scale = jnp.broadcast_to(k_scale, (HEAD_DIM, half_rows)).T
        cosines, sines = cosine_ref[...], sine_ref[...]

        def rotated(lower, scale, gain):
            field = total_ref[:, lower : lower + HEAD_DIM] * scale * gain
            return (
                field * cosines + pltpu.roll(field, HEAD_DIM // 2, 1) * sines
            ).astype(jnp.bfloat16)

        for g in range(kv_heads):
            low = g * HEAD_DIM
            keys = rotated(q_width + low, k_scale, k_gain_ref[:, low : low + HEAD_DIM])
            values = total_ref[:, q_width + k_width + low : q_width + k_width + low + HEAD_DIM]
            values = values.astype(jnp.bfloat16)
            queries = []
            for h in range(g * group, (g + 1) * group):
                span = slice(h * HEAD_DIM, (h + 1) * HEAD_DIM)
                queries.append(rotated(h * HEAD_DIM, q_scale, q_gain_ref[:, span]))
            for i in range(half_rows // block):
                lower, reach = i * block, (i + 1) * block
                stacked = jnp.concatenate([q[lower:reach] for q in queries], axis=0)
                scores = lax.dot_general(
                    stacked,
                    keys[:reach],
                    (((1,), (1,)), ((), ())),
                    preferred_element_type=jnp.float32,
                ) * (1.0 / math.sqrt(HEAD_DIM))
                first = starts_ref[lower:reach, :] - offset
                lanes = lax.broadcasted_iota(jnp.int32, (block, block), 1)
                row = lax.broadcasted_iota(jnp.int32, (block, block), 0)
                allowed = jnp.concatenate(
                    [lanes + c * block >= first for c in range(i)]
                    + [(lanes + lower >= first) & (lanes <= row)],
                    axis=1,
                )
                scores = scores.reshape(group, block, reach)
                scores = jnp.where(allowed[None], scores, jnp.float32(-1e30))
                peak = jnp.max(scores, axis=-1, keepdims=True)
                expo = jnp.exp(scores - peak)
                probs = expo / jnp.sum(expo, axis=-1, keepdims=True)
                probs = probs.astype(jnp.bfloat16).reshape(group * block, reach)
                mixed = jnp.dot(probs, values[:reach], preferred_element_type=jnp.float32)
                mixed = mixed.astype(jnp.bfloat16)
                for h in range(group):
                    column = (g * group + h) * HEAD_DIM
                    out_ref[lower:reach, column : column + HEAD_DIM] = mixed[
                        h * block : (h + 1) * block
                    ]

    def by_rows(width):
        return pl.BlockSpec((half_rows, width), lambda i: (i, 0))

    def constant(width):
        return pl.BlockSpec((1, width), lambda i: (0, 0))

    return pl.pallas_call(
        kernel,
        grid=(capacity // half_rows,),
        out_shape=jax.ShapeDtypeStruct((capacity, q_width), jnp.bfloat16),
        in_specs=[by_rows(total.shape[1])]
        + [pl.BlockSpec((8, half_rows), lambda i: (0, i))] * len(sums)
        + [by_rows(HEAD_DIM)] * 3
        + [constant(q_width), constant(k_width)],
        out_specs=by_rows(q_width),
        compiler_params=pltpu.CompilerParams(vmem_limit_bytes=24 * 2**20),
        cost_estimate=pl.CostEstimate(
            flops=4 * capacity * half_rows * q_width,
            bytes_accessed=8 * capacity * total.shape[1],
            transcendentals=capacity * half_rows * heads,
        ),
    )(total, *sums, cosine, sine, starts, query_gain, key_gain)


def finish(attn_out, sums, tokens, out_gain, live_rows, features):
    rows, width = tokens.shape
    tile = 256 if rows % 256 == 0 else rows

    def kernel(*refs):
        live_ref, attn_ref, sum_refs = refs[0], refs[1], refs[2 : 2 + len(sums)]
        tokens_ref, gain_ref, out_ref = refs[2 + len(sums) :]
        squares = sum_refs[0][...]
        for other in sum_refs[1:]:
            squares = squares + other[...]
        scale = lax.rsqrt(squares[0:1] / features + EPS)
        scale = jnp.broadcast_to(scale, (128, tile)).T
        row = pl.program_id(0) * tile + lax.broadcasted_iota(jnp.int32, (tile, 128), 0)
        live = row < live_ref[0]
        for lower in range(0, width, 128):
            span = slice(lower, lower + 128)
            value = tokens_ref[:, span].astype(jnp.float32) + attn_ref[:, span] * scale * gain_ref[:, span]
            out_ref[:, span] = jnp.where(live, value, 0.0).astype(jnp.bfloat16)

    return pl.pallas_call(
        kernel,
        grid=(rows // tile,),
        out_shape=jax.ShapeDtypeStruct((rows, width), jnp.bfloat16),
        in_specs=[
            pl.BlockSpec(memory_space=pltpu.SMEM),
            pl.BlockSpec((tile, width), lambda i: (i, 0)),
        ]
        + [pl.BlockSpec((8, tile), lambda i: (0, i))] * len(sums)
        + [
            pl.BlockSpec((tile, width), lambda i: (i, 0)),
            pl.BlockSpec((1, width), lambda i: (0, 0)),
        ],
        out_specs=pl.BlockSpec((tile, width), lambda i: (i, 0)),
        compiler_params=pltpu.CompilerParams(vmem_limit_bytes=16 * 2**20),
    )(live_rows, attn_out, *sums, tokens, out_gain)


def body(
    sizes, tokens, live_rows, first_row, w_query, w_key, w_value, w_out, query_gain, key_gain, out_gain
):
    n, tensor_size = sizes
    capacity, width = tokens.shape
    half_rows = capacity // 2
    per_tensor = n // tensor_size

    depth = w_query.shape[0]
    columns = w_query.shape[1] + w_key.shape[1] + w_value.shape[1]
    top, bottom = pack_weights([w_query, w_key, w_value])
    moved = permute(
        w_out,
        sizes,
        lambda f, t: (
            ((f // per_tensor) ^ reverse_bits(t, tensor_size)) * per_tensor + f % per_tensor,
            t,
        ),
    )
    local_tokens, top, bottom = lax.optimization_barrier((tokens, top, bottom))
    token_blocks = gather_tensor(local_tokens, sizes)
    ties = {2: lambda *_: moved}
    tops, bottoms = ring_gather(top, bottom, sizes, ties)
    moved = ties[2]
    moved = permute(
        moved, sizes, lambda f, t: (f, (f // per_tensor) ^ reverse_bits(t, tensor_size))
    )

    q_width, k_width = w_query.shape[1], w_key.shape[1]
    steps = [[0, n // 2]] + [[s, n - s] for s in range(n // 2 + 1, n)]
    middle = (len(steps) + 1) // 2
    groups = [[offset for group in steps[:middle] for offset in group]] + steps[middle:]

    def choose_tokens(offset):
        block = snake_block(sizes, lax.axis_index("fsdp"), offset)
        which = (block // per_tensor) ^ lax.axis_index("tensor")
        return which, lax.rem(block, per_tensor) * depth, 0

    total = None
    for number, offsets in enumerate(groups):
        total = block_product(
            sizes,
            token_blocks,
            choose_tokens,
            offsets,
            tops,
            bottoms,
            total,
            columns,
            [(0, q_width), (q_width, q_width + k_width)] if number == len(groups) - 1 else None,
        )
    total, squares = total

    out_half = w_out.shape[0] // 2
    out_top, out_bottom, _ = lax.optimization_barrier(
        (moved[:out_half], moved[out_half:], (tops[-1], bottoms[-1]))
    )
    square_blocks = swap_small(squares, sizes)
    row_ids = jnp.arange(capacity, dtype=jnp.int32)
    positions = (row_ids - first_row).astype(jnp.float32)
    half_dim = HEAD_DIM // 2
    freqs = jnp.power(
        ROPE_BASE, -(jnp.arange(half_dim, dtype=jnp.float32) * 2.0 / HEAD_DIM)
    )
    angle = positions[:, None] * freqs[None, :]
    cosine, sine = jnp.cos(angle), jnp.sin(angle)
    attended = attention(
        total,
        square_blocks,
        jnp.concatenate([cosine, cosine], axis=1),
        jnp.concatenate([-sine, sine], axis=1),
        jnp.broadcast_to(first_row[:, None], (capacity, HEAD_DIM)),
        query_gain[None, :],
        key_gain[None, :],
        tensor_size,
        half_rows,
    )
    attended_blocks = gather_tensor(attended, sizes)

    def choose_attended(offset):
        block = snake_block(sizes, lax.axis_index("fsdp"), offset)
        t_index = lax.axis_index("tensor")
        source = traced_reverse((block // per_tensor) ^ t_index, tensor_size)
        return source ^ t_index, 0, lax.rem(block, per_tensor) * w_out.shape[1]

    def out_product(number, out_tops, out_bottoms, attn_out):
        return block_product(
            sizes,
            attended_blocks,
            choose_attended,
            groups[number],
            out_tops,
            out_bottoms,
            attn_out,
            width,
            [(0, width)] if number == len(groups) - 1 else None,
        )

    ready = max(groups[0])
    ties = {ready + 1: lambda now_tops, now_bottoms: out_product(0, now_tops, now_bottoms, None)}
    out_tops, out_bottoms = ring_gather(out_top, out_bottom, sizes, ties)
    attn_out = ties[ready + 1]
    for number in range(1, len(groups)):
        attn_out = out_product(number, out_tops, out_bottoms, attn_out)
    attn_out, out_squares = attn_out
    return finish(
        attn_out,
        swap_small(out_squares, sizes),
        tokens,
        out_gain[None, :],
        live_rows,
        width * tensor_size,
    )


def solution(mesh):
    sizes = (mesh.shape["fsdp"], mesh.shape["tensor"])

    def run(*arrays):
        return body(sizes, *arrays)

    in_specs = (
        P("fsdp", "tensor"),
        P("fsdp"),
        P("fsdp"),
        P("fsdp", "tensor"),
        P("fsdp", "tensor"),
        P("fsdp", "tensor"),
        P("tensor", "fsdp"),
        P("tensor"),
        P("tensor"),
        P("tensor"),
    )
    return jax.shard_map(
        run, mesh=mesh, in_specs=in_specs, out_specs=P("fsdp", "tensor"), check_vma=False
    )
```

```python
import math

import jax
import jax.numpy as jnp
from jax import lax
from jax.experimental import pallas as pl
from jax.experimental.pallas import tpu as pltpu
from jax.sharding import PartitionSpec as P

HEAD_DIM = 128
EPS = 1e-06
ROPE_BASE = 500000.0
AXES = ("fsdp", "tensor")


def permute(array, mesh_sizes, target):
    n, tensor_size = mesh_sizes
    pairs = []
    for f in range(n):
        for t in range(tensor_size):
            to_f, to_t = target(f, t)
            pairs.append((f * tensor_size + t, to_f * tensor_size + to_t))
    return lax.ppermute(array, AXES, pairs)


def reverse_bits(value, size):
    result = 0
    while size > 1:
        result = result * 2 + value % 2
        value //= 2
        size //= 2
    return result


def snake(n):
    return list(range(0, n, 2)) + list(range(n - 1, 0, -2))


def gather_first(array, sizes):
    half = sizes[1] // 2
    return {0: [array], half: [permute(array, sizes, lambda f, t: (f, t ^ half))]}


def gather_rest(have, sizes):
    bit = sizes[1] // 4
    while bit:
        for r in sorted(have):
            have[r ^ bit] = [
                permute(part, sizes, lambda f, t, bit=bit: (f, t ^ bit)) for part in have[r]
            ]
        bit //= 2
    return [have[r] for r in range(sizes[1])]


def swap_small(array, sizes):
    return [array] + [
        permute(array, sizes, lambda f, t, r=r: (f, t ^ r)) for r in range(1, sizes[1])
    ]


def ring_open(array):
    return {"forward": [array], "backward": [array]}


def ring_send(arrays, sizes):
    n = sizes[0]
    order = snake(n)
    place = {f: i for i, f in enumerate(order)}
    return [
        permute(array, sizes, lambda f, t: (order[(place[f] + way) % n], t))
        for array, way in zip(arrays, (1, -1))
    ]


def ring_step(ring, sizes):
    arrived = ring_send((ring["forward"][-1], ring["backward"][-1]), sizes)
    ring["forward"].append(arrived[0])
    ring["backward"].append(arrived[1])


def ring_middle(ring, sizes):
    forward, backward = ring["forward"][-1], ring["backward"][-1]
    half = forward.shape[0] // 2
    ring["middle"] = ring_send((forward[:half], backward[half:]), sizes)


def ring_end(ring, sizes, between):
    forward, backward = ring["forward"][-1], ring["backward"][-1]
    half = forward.shape[0] // 2
    ahead = ring_send((forward[:half], backward[half:]), sizes)
    rest, ahead = lax.optimization_barrier(((forward[half:], backward[:half]), ahead))
    rest = ring_send(rest, sizes)
    ring["forward"].append([ahead[0], rest[0]])
    ring["backward"].append([rest[1], ahead[1]])
    ahead, result = lax.optimization_barrier((ahead, between(ahead)))
    halves = ring_send(ahead, sizes)
    ring["middle"] = halves
    return result


def ring_tie(ring, other):
    ring["forward"][-1], ring["backward"][-1], other = lax.optimization_barrier(
        (ring["forward"][-1], ring["backward"][-1], other)
    )
    return other


def ring_block(ring, offset, n):
    if 2 * offset == n:
        return ring["middle"]
    block = ring["backward"][offset] if 2 * offset < n else ring["forward"][n - offset]
    return block if isinstance(block, list) else [block]


def snake_block(sizes, f_index, offset):
    n = sizes[0]
    ahead = lax.rem(f_index, 2) == 0
    position = jnp.where(ahead, f_index // 2, n - 1 - f_index // 2)
    place = lax.rem(position + offset, n)
    return jnp.where(place < (n + 1) // 2, 2 * place, 2 * (n - place) - 1)


def traced_reverse(value, size):
    result = value * 0
    while size > 1:
        result = result * 2 + lax.rem(value, 2)
        value = value // 2
        size //= 2
    return result


def block_product(sources, choose, matrices, accumulated, columns, spans):
    rows = sum(part.shape[0] for part in sources[0])
    offsets = list(matrices)
    chunks = [matrices[key] for key in offsets]
    width = chunks[0][0].shape[1]
    depth = sum(chunk.shape[0] for chunk in chunks[0])
    parts = sum(len(block) for block in chunks)
    count = len(chunks)
    if depth % 128 or width % 128:
        stack = jnp.stack([jnp.concatenate(source, axis=0) for source in sources])
        total = jnp.zeros((rows, columns), jnp.float32) if accumulated is None else accumulated
        for j in range(count):
            which, first, column = choose(offsets[j])
            piece = lax.dynamic_slice(stack, (which, 0, first), (1, rows, depth))[0]
            matrix = jnp.concatenate(chunks[j], axis=0)
            term = jnp.dot(piece, matrix, preferred_element_type=jnp.float32)
            current = lax.dynamic_slice(total, (0, column), (rows, width))
            total = lax.dynamic_update_slice(total, current + term, (0, column))
        if spans is None:
            return total
        squares = [jnp.sum(total[:, low:high] ** 2, axis=1) for low, high in spans]
        squares += [jnp.zeros_like(squares[0])] * (8 - len(squares))
        return total, jnp.stack(squares)

    tile = 256 if rows % 256 == 0 else rows
    tiles = rows // tile
    extra = 0 if accumulated is None else 1
    whole = width == columns

    def kernel(*refs):
        held = sum(len(source) for source in sources)
        source, refs = list(refs[:held]), refs[held:]
        source = [[source.pop(0) for _ in each] for each in sources]
        pieces, refs = list(refs[:parts]), refs[parts:]
        pieces = [[pieces.pop(0) for _ in block] for block in chunks]
        start, refs = refs[:extra], refs[extra:]
        out, refs = refs[0], refs[1:]
        squares, refs = refs[: spans is not None], refs[spans is not None :]
        piece, matrix, total, sems, tile_sems = refs
        choices = [choose(offset) for offset in offsets]

        def piece_copy(j, part, lower):
            first = choices[j][1]
            if not isinstance(first, int):
                first = pl.multiple_of(first, 128)
            return pltpu.make_async_copy(
                part.at[:, pl.ds(first, depth)],
                piece.at[pl.ds(lower, part.shape[0]), pl.ds(j * depth, depth)],
                sems.at[j, 0],
            )

        def matrix_copies(j):
            rows_each = depth // len(pieces[j])
            return [
                pltpu.make_async_copy(
                    part,
                    matrix.at[pl.ds(j * depth + k * rows_each, rows_each)],
                    sems.at[j, 1 + k],
                )
                for k, part in enumerate(pieces[j])
            ]

        def in_copy(i):
            part = pl.ds(i * tile, tile)
            return pltpu.make_async_copy(start[0].at[part], total.at[part], tile_sems.at[i, 0])

        def out_copy(i):
            part = pl.ds(i * tile, tile)
            return pltpu.make_async_copy(total.at[part], out.at[part], tile_sems.at[i, 1])

        for j in range(count):
            for which in range(len(sources)):

                @pl.when(choices[j][0] == which)
                def _(j=j, which=which):
                    lower = 0
                    for part in source[which]:
                        piece_copy(j, part, lower).start()
                        lower += part.shape[0]

            for copy in matrix_copies(j):
                copy.start()
        for i in range(tiles * extra):
            in_copy(i).start()
        together = 2 if whole else 1
        for low in range(0, count, together):
            blocks = range(low, min(low + together, count))
            for j in blocks:
                everything = piece.at[:, pl.ds(j * depth, depth)]
                pltpu.make_async_copy(everything, everything, sems.at[j, 0]).wait()
                for copy in matrix_copies(j):
                    copy.wait()
            span = pl.ds(low * depth, len(blocks) * depth)
            for i in range(tiles):
                part = pl.ds(i * tile, tile)
                if low == 0 and extra:
                    in_copy(i).wait()
                if low == 0 and not extra and not whole:
                    total[part, :] = jnp.zeros((tile, columns), jnp.float32)
                term = jnp.dot(piece[part, span], matrix[span, :], preferred_element_type=jnp.float32)
                if whole:
                    total[part, :] = total[part, :] + term if extra or low else term
                else:
                    total[part, pl.ds(pl.multiple_of(choices[low][2], 128), width)] += term
                if blocks[-1] < count - 1:
                    continue
                out_copy(i).start()
                if spans is not None:
                    sums = []
                    for first, last in spans:
                        chosen = total[part, first:last]
                        chosen = jnp.sum(chosen * chosen, axis=1, keepdims=True)
                        sums.append(jnp.broadcast_to(chosen, (tile, 128)).T[:8])
                    lines = lax.broadcasted_iota(jnp.int32, (8, tile), 0)
                    line = sums[0]
                    for index in range(1, len(sums)):
                        line = jnp.where(lines == index, sums[index], line)
                    squares[0][:, part] = line
        for i in range(tiles):
            out_copy(i).wait()

    any_space = pl.BlockSpec(memory_space=pl.ANY)
    out_shape = [jax.ShapeDtypeStruct((rows, columns), jnp.float32)]
    out_specs = [any_space]
    if spans is not None:
        out_shape.append(jax.ShapeDtypeStruct((8, rows), jnp.float32))
        out_specs.append(pl.BlockSpec(memory_space=pltpu.VMEM))
    operands = [*sum(sources, []), *sum(chunks, [])] + [accumulated] * extra
    needed = 2 * count * depth * (rows + width) + 4 * rows * columns
    results = pl.pallas_call(
        kernel,
        out_shape=out_shape,
        in_specs=[any_space] * len(operands),
        out_specs=out_specs,
        scratch_shapes=[
            pltpu.VMEM((rows, count * depth), sources[0][0].dtype),
            pltpu.VMEM((count * depth, width), chunks[0][0].dtype),
            pltpu.VMEM((rows, columns), jnp.float32),
            pltpu.SemaphoreType.DMA((count, 1 + max(len(block) for block in chunks))),
            pltpu.SemaphoreType.DMA((tiles, 2)),
        ],
        compiler_params=pltpu.CompilerParams(vmem_limit_bytes=needed + 6 * 2**20),
        cost_estimate=pl.CostEstimate(flops=1, bytes_accessed=1, transcendentals=0),
    )(*operands)
    return tuple(results) if spans is not None else results[0]


def attention(total, sums, cosine, sine, starts, query_gain, key_gain, tensor_size, half_rows):
    capacity = total.shape[0]
    q_width, k_width = query_gain.shape[1], key_gain.shape[1]
    heads, kv_heads = q_width // HEAD_DIM, k_width // HEAD_DIM
    group = heads // kv_heads
    block = 128

    def kernel(*refs):
        total_ref, sum_refs = refs[0], refs[1 : 1 + len(sums)]
        cosine_ref, sine_ref, starts_ref, q_gain_ref, k_gain_ref, out_ref = refs[1 + len(sums) :]
        offset = pl.program_id(0) * half_rows
        squares = sum_refs[0][...]
        for other in sum_refs[1:]:
            squares = squares + other[...]
        q_scale = lax.rsqrt(squares[0:1] / (q_width * tensor_size) + EPS)
        k_scale = lax.rsqrt(squares[1:2] / (k_width * tensor_size) + EPS)
        q_scale = jnp.broadcast_to(q_scale, (HEAD_DIM, half_rows)).T
        k_scale = jnp.broadcast_to(k_scale, (HEAD_DIM, half_rows)).T
        cosines, sines = cosine_ref[...], sine_ref[...]

        def rotated(lower, scale, gain):
            field = total_ref[:, lower : lower + HEAD_DIM] * scale * gain
            return (
                field * cosines + pltpu.roll(field, HEAD_DIM // 2, 1) * sines
            ).astype(jnp.bfloat16)

        for g in range(kv_heads):
            low = g * HEAD_DIM
            keys = rotated(q_width + low, k_scale, k_gain_ref[:, low : low + HEAD_DIM])
            values = total_ref[:, q_width + k_width + low : q_width + k_width + low + HEAD_DIM]
            values = values.astype(jnp.bfloat16)
            queries = []
            for h in range(g * group, (g + 1) * group):
                span = slice(h * HEAD_DIM, (h + 1) * HEAD_DIM)
                queries.append(rotated(h * HEAD_DIM, q_scale, q_gain_ref[:, span]))
            for i in range(half_rows // block):
                lower, reach = i * block, (i + 1) * block
                stacked = jnp.concatenate([q[lower:reach] for q in queries], axis=0)
                scores = lax.dot_general(
                    stacked,
                    keys[:reach],
                    (((1,), (1,)), ((), ())),
                    preferred_element_type=jnp.float32,
                ) * (1.0 / math.sqrt(HEAD_DIM))
                first = starts_ref[lower:reach, :] - offset
                lanes = lax.broadcasted_iota(jnp.int32, (block, block), 1)
                row = lax.broadcasted_iota(jnp.int32, (block, block), 0)
                allowed = jnp.concatenate(
                    [lanes + c * block >= first for c in range(i)]
                    + [(lanes + lower >= first) & (lanes <= row)],
                    axis=1,
                )
                scores = scores.reshape(group, block, reach)
                scores = jnp.where(allowed[None], scores, jnp.float32(-1e30))
                peak = jnp.max(scores, axis=-1, keepdims=True)
                expo = jnp.exp(scores - peak)
                probs = expo / jnp.sum(expo, axis=-1, keepdims=True)
                probs = probs.astype(jnp.bfloat16).reshape(group * block, reach)
                mixed = jnp.dot(probs, values[:reach], preferred_element_type=jnp.float32)
                mixed = mixed.astype(jnp.bfloat16)
                for h in range(group):
                    column = (g * group + h) * HEAD_DIM
                    out_ref[lower:reach, column : column + HEAD_DIM] = mixed[
                        h * block : (h + 1) * block
                    ]

    def by_rows(width):
        return pl.BlockSpec((half_rows, width), lambda i: (i, 0))

    def constant(width):
        return pl.BlockSpec((1, width), lambda i: (0, 0))

    return pl.pallas_call(
        kernel,
        grid=(capacity // half_rows,),
        out_shape=jax.ShapeDtypeStruct((capacity, q_width), jnp.bfloat16),
        in_specs=[by_rows(total.shape[1])]
        + [pl.BlockSpec((8, half_rows), lambda i: (0, i))] * len(sums)
        + [by_rows(HEAD_DIM)] * 3
        + [constant(q_width), constant(k_width)],
        out_specs=by_rows(q_width),
        compiler_params=pltpu.CompilerParams(vmem_limit_bytes=24 * 2**20),
        cost_estimate=pl.CostEstimate(flops=1, bytes_accessed=1, transcendentals=0),
    )(total, *sums, cosine, sine, starts, query_gain, key_gain)


def finish(attn_out, sums, tokens, out_gain, live_rows, features):
    rows, width = tokens.shape
    tile = 256 if rows % 256 == 0 else rows

    def kernel(*refs):
        live_ref, attn_ref, sum_refs = refs[0], refs[1], refs[2 : 2 + len(sums)]
        tokens_ref, gain_ref, out_ref = refs[2 + len(sums) :]
        squares = sum_refs[0][...]
        for other in sum_refs[1:]:
            squares = squares + other[...]
        scale = lax.rsqrt(squares[0:1] / features + EPS)
        scale = jnp.broadcast_to(scale, (128, tile)).T
        row = pl.program_id(0) * tile + lax.broadcasted_iota(jnp.int32, (tile, 128), 0)
        live = row < live_ref[0]
        for lower in range(0, width, 128):
            span = slice(lower, lower + 128)
            value = tokens_ref[:, span].astype(jnp.float32) + attn_ref[:, span] * scale * gain_ref[:, span]
            out_ref[:, span] = jnp.where(live, value, 0.0).astype(jnp.bfloat16)

    return pl.pallas_call(
        kernel,
        grid=(rows // tile,),
        out_shape=jax.ShapeDtypeStruct((rows, width), jnp.bfloat16),
        in_specs=[
            pl.BlockSpec(memory_space=pltpu.SMEM),
            pl.BlockSpec((tile, width), lambda i: (i, 0)),
        ]
        + [pl.BlockSpec((8, tile), lambda i: (0, i))] * len(sums)
        + [
            pl.BlockSpec((tile, width), lambda i: (i, 0)),
            pl.BlockSpec((1, width), lambda i: (0, 0)),
        ],
        out_specs=pl.BlockSpec((tile, width), lambda i: (i, 0)),
        compiler_params=pltpu.CompilerParams(vmem_limit_bytes=16 * 2**20),
    )(live_rows, attn_out, *sums, tokens, out_gain)


def body(
    sizes, tokens, live_rows, first_row, w_query, w_key, w_value, w_out, query_gain, key_gain, out_gain
):
    n, tensor_size = sizes
    capacity, width = tokens.shape
    half_rows = capacity // 2
    per_tensor = n // tensor_size

    depth = w_query.shape[0]
    columns = w_query.shape[1] + w_key.shape[1] + w_value.shape[1]
    last = n // 2
    groups = [
        [0] + [offset for step in range(1, last - 1) for offset in (step, n - step)],
        [last - 1, n - last + 1],
        [last],
    ]

    moved = permute(
        w_out,
        sizes,
        lambda f, t: (
            ((f // per_tensor) ^ reverse_bits(t, tensor_size)) * per_tensor + f % per_tensor,
            t,
        ),
    )
    token_blocks = gather_first(tokens, sizes)
    weights = jnp.concatenate([w_query, w_key, w_value], axis=1)
    first_ring = ring_open(weights)
    q_width, k_width = w_query.shape[1], w_key.shape[1]

    def choose_tokens(offset):
        block = snake_block(sizes, lax.axis_index("fsdp"), offset)
        which = (block // per_tensor) ^ lax.axis_index("tensor")
        return which, lax.rem(block, per_tensor) * depth, 0

    def qkv_product(number, total):
        return block_product(
            token_blocks,
            choose_tokens,
            {offset: ring_block(first_ring, offset, n) for offset in groups[number]},
            total,
            columns,
            [(0, q_width), (q_width, q_width + k_width)] if number == len(groups) - 1 else None,
        )

    for step in range(1, last - 1):
        ring_step(first_ring, sizes)
        if step == 1:
            token_blocks, moved = ring_tie(first_ring, (token_blocks, moved))
            token_blocks = gather_rest(token_blocks, sizes)
            moved = permute(
                moved, sizes, lambda f, t: (f, (f // per_tensor) ^ reverse_bits(t, tensor_size))
            )
    ring_step(first_ring, sizes)
    total, moved = ring_tie(first_ring, (qkv_product(0, None), moved))
    ring_middle(first_ring, sizes)
    for number in range(1, len(groups) - 1):
        total = qkv_product(number, total)
    moved, total, _ = lax.optimization_barrier(
        (moved, total, first_ring["middle"])
    )
    total, squares = qkv_product(len(groups) - 1, total)

    second_ring = ring_open(moved)
    ring_step(second_ring, sizes)
    square_blocks = swap_small(squares, sizes)
    row_ids = jnp.arange(capacity, dtype=jnp.int32)
    positions = (row_ids - first_row).astype(jnp.float32)
    half_dim = HEAD_DIM // 2
    freqs = jnp.power(
        ROPE_BASE, -(jnp.arange(half_dim, dtype=jnp.float32) * 2.0 / HEAD_DIM)
    )
    angle = positions[:, None] * freqs[None, :]
    cosine, sine = jnp.cos(angle), jnp.sin(angle)
    attended = attention(
        total,
        square_blocks,
        jnp.concatenate([cosine, cosine], axis=1),
        jnp.concatenate([-sine, sine], axis=1),
        jnp.broadcast_to(first_row[:, None], (capacity, HEAD_DIM)),
        query_gain[None, :],
        key_gain[None, :],
        tensor_size,
        half_rows,
    )
    attended_blocks = gather_first(attended, sizes)
    ring_tie(second_ring, attended)

    def choose_attended(offset):
        block = snake_block(sizes, lax.axis_index("fsdp"), offset)
        t_index = lax.axis_index("tensor")
        source = traced_reverse((block // per_tensor) ^ t_index, tensor_size)
        return source ^ t_index, 0, lax.rem(block, per_tensor) * w_out.shape[1]

    def out_product(number, sources, attn_out):
        return block_product(
            sources,
            choose_attended,
            {offset: ring_block(second_ring, offset, n) for offset in groups[number]},
            attn_out,
            width,
            [(0, width)] if number == len(groups) - 1 else None,
        )

    for step in range(2, last - 1):
        ring_step(second_ring, sizes)

    def first_product(ahead):
        have, _ = lax.optimization_barrier((attended_blocks, ahead))
        have = gather_rest(have, sizes)
        return have, out_product(0, have, None)

    attended_blocks, attn_out = ring_end(second_ring, sizes, first_product)
    for number in range(1, len(groups)):
        attn_out = out_product(number, attended_blocks, attn_out)
    attn_out, out_squares = attn_out
    return finish(
        attn_out,
        swap_small(out_squares, sizes),
        tokens,
        out_gain[None, :],
        live_rows,
        width * tensor_size,
    )


def solution(mesh):
    sizes = (mesh.shape["fsdp"], mesh.shape["tensor"])

    def run(*arrays):
        return body(sizes, *arrays)

    in_specs = (
        P("fsdp", "tensor"),
        P("fsdp"),
        P("fsdp"),
        P("fsdp", "tensor"),
        P("fsdp", "tensor"),
        P("fsdp", "tensor"),
        P("tensor", "fsdp"),
        P("tensor"),
        P("tensor"),
        P("tensor"),
    )
    return jax.shard_map(
        run, mesh=mesh, in_specs=in_specs, out_specs=P("fsdp", "tensor"), check_vma=False
    )
```

```python
import math

import jax
import jax.numpy as jnp
from jax import lax
from jax.experimental import pallas as pl
from jax.experimental.pallas import tpu as pltpu
from jax.sharding import PartitionSpec as P

HEAD_DIM = 128
EPS = 1e-06
ROPE_BASE = 500000.0
AXES = ("fsdp", "tensor")


def permute(array, mesh_sizes, target):
    n, tensor_size = mesh_sizes
    pairs = []
    for f in range(n):
        for t in range(tensor_size):
            to_f, to_t = target(f, t)
            pairs.append((f * tensor_size + t, to_f * tensor_size + to_t))
    return lax.ppermute(array, AXES, pairs)


def reverse_bits(value, size):
    result = 0
    while size > 1:
        result = result * 2 + value % 2
        value //= 2
        size //= 2
    return result


def snake(n):
    return list(range(0, n, 2)) + list(range(n - 1, 0, -2))


def gather_first(array, sizes):
    half = sizes[1] // 2
    return {0: [array], half: [permute(array, sizes, lambda f, t: (f, t ^ half))]}


def gather_rest(have, sizes):
    bit = sizes[1] // 4
    while bit:
        for r in sorted(have):
            have[r ^ bit] = [
                permute(part, sizes, lambda f, t, bit=bit: (f, t ^ bit)) for part in have[r]
            ]
        bit //= 2
    return [have[r] for r in range(sizes[1])]


def swap_small(array, sizes):
    return [array] + [
        permute(array, sizes, lambda f, t, r=r: (f, t ^ r)) for r in range(1, sizes[1])
    ]


def ring_open(array):
    return {"forward": [array], "backward": [array]}


def ring_send(arrays, sizes):
    n = sizes[0]
    order = snake(n)
    place = {f: i for i, f in enumerate(order)}
    return [
        permute(array, sizes, lambda f, t: (order[(place[f] + way) % n], t))
        for array, way in zip(arrays, (1, -1))
    ]


def ring_step(ring, sizes):
    arrived = ring_send((ring["forward"][-1], ring["backward"][-1]), sizes)
    ring["forward"].append(arrived[0])
    ring["backward"].append(arrived[1])


def ring_middle(ring, sizes):
    forward, backward = ring["forward"][-1], ring["backward"][-1]
    half = forward.shape[0] // 2
    ring["middle"] = ring_send((forward[:half], backward[half:]), sizes)


def ring_tie(ring, other):
    ring["forward"][-1], ring["backward"][-1], other = lax.optimization_barrier(
        (ring["forward"][-1], ring["backward"][-1], other)
    )
    return other


def ring_block(ring, offset, n):
    if 2 * offset == n:
        return ring["middle"]
    block = ring["backward"][offset] if 2 * offset < n else ring["forward"][n - offset]
    return block if isinstance(block, list) else [block]


def snake_block(sizes, f_index, offset):
    n = sizes[0]
    ahead = lax.rem(f_index, 2) == 0
    position = jnp.where(ahead, f_index // 2, n - 1 - f_index // 2)
    place = lax.rem(position + offset, n)
    return jnp.where(place < (n + 1) // 2, 2 * place, 2 * (n - place) - 1)


def traced_reverse(value, size):
    result = value * 0
    while size > 1:
        result = result * 2 + lax.rem(value, 2)
        value = value // 2
        size //= 2
    return result


def block_product(sources, choose, matrices, accumulated, columns, spans):
    rows = sum(part.shape[0] for part in sources[0])
    offsets = list(matrices)
    chunks = [matrices[key] for key in offsets]
    width = chunks[0][0].shape[1]
    depth = sum(chunk.shape[0] for chunk in chunks[0])
    parts = sum(len(block) for block in chunks)
    count = len(chunks)
    if depth % 128 or width % 128:
        stack = jnp.stack([jnp.concatenate(source, axis=0) for source in sources])
        total = jnp.zeros((rows, columns), jnp.float32) if accumulated is None else accumulated
        for j in range(count):
            which, first, column = choose(offsets[j])
            piece = lax.dynamic_slice(stack, (which, 0, first), (1, rows, depth))[0]
            matrix = jnp.concatenate(chunks[j], axis=0)
            term = jnp.dot(piece, matrix, preferred_element_type=jnp.float32)
            current = lax.dynamic_slice(total, (0, column), (rows, width))
            total = lax.dynamic_update_slice(total, current + term, (0, column))
        if spans is None:
            return total
        squares = [jnp.sum(total[:, low:high] ** 2, axis=1) for low, high in spans]
        squares += [jnp.zeros_like(squares[0])] * (8 - len(squares))
        return total, jnp.stack(squares)

    extra = 0 if accumulated is None else 1
    whole = width == columns
    tile = 384 if whole else 256
    tile = tile if rows % tile == 0 else rows
    tiles = rows // tile

    def kernel(*refs):
        held = sum(len(source) for source in sources)
        source, refs = list(refs[:held]), refs[held:]
        source = [[source.pop(0) for _ in each] for each in sources]
        pieces, refs = list(refs[:parts]), refs[parts:]
        pieces = [[pieces.pop(0) for _ in block] for block in chunks]
        start, refs = refs[:extra], refs[extra:]
        out, refs = refs[0], refs[1:]
        squares, refs = refs[: spans is not None], refs[spans is not None :]
        piece, matrix, total, sems, tile_sems = refs
        choices = [choose(offset) for offset in offsets]

        def piece_copy(j, part, lower):
            first = choices[j][1]
            if not isinstance(first, int):
                first = pl.multiple_of(first, 128)
            return pltpu.make_async_copy(
                part.at[:, pl.ds(first, depth)],
                piece.at[pl.ds(lower, part.shape[0]), pl.ds(j * depth, depth)],
                sems.at[j, 0],
            )

        def matrix_copies(j):
            rows_each = depth // len(pieces[j])
            return [
                pltpu.make_async_copy(
                    part,
                    matrix.at[pl.ds(j * depth + k * rows_each, rows_each)],
                    sems.at[j, 1 + k],
                )
                for k, part in enumerate(pieces[j])
            ]

        def in_copy(i):
            part = pl.ds(i * tile, tile)
            return pltpu.make_async_copy(start[0].at[part], total.at[part], tile_sems.at[i, 0])

        def out_copy(i):
            part = pl.ds(i * tile, tile)
            return pltpu.make_async_copy(total.at[part], out.at[part], tile_sems.at[i, 1])

        for j in range(count):
            for which in range(len(sources)):

                @pl.when(choices[j][0] == which)
                def _(j=j, which=which):
                    lower = 0
                    for part in source[which]:
                        piece_copy(j, part, lower).start()
                        lower += part.shape[0]

            for copy in matrix_copies(j):
                copy.start()
        for i in range(tiles * extra):
            in_copy(i).start()
        together = 2 if whole else 1
        for low in range(0, count, together):
            blocks = range(low, min(low + together, count))
            for j in blocks:
                everything = piece.at[:, pl.ds(j * depth, depth)]
                pltpu.make_async_copy(everything, everything, sems.at[j, 0]).wait()
                for copy in matrix_copies(j):
                    copy.wait()
            span = pl.ds(low * depth, len(blocks) * depth)
            for i in range(tiles):
                part = pl.ds(i * tile, tile)
                if low == 0 and extra:
                    in_copy(i).wait()
                if low == 0 and not extra and not whole:
                    total[part, :] = jnp.zeros((tile, columns), jnp.float32)
                term = jnp.dot(piece[part, span], matrix[span, :], preferred_element_type=jnp.float32)
                if whole:
                    total[part, :] = total[part, :] + term if extra or low else term
                else:
                    total[part, pl.ds(pl.multiple_of(choices[low][2], 128), width)] += term
                if blocks[-1] < count - 1:
                    continue
                out_copy(i).start()
                if spans is not None:
                    sums = []
                    for first, last in spans:
                        chosen = total[part, first:last]
                        chosen = jnp.sum(chosen * chosen, axis=1, keepdims=True)
                        sums.append(jnp.broadcast_to(chosen, (tile, 128)).T[:8])
                    lines = lax.broadcasted_iota(jnp.int32, (8, tile), 0)
                    line = sums[0]
                    for index in range(1, len(sums)):
                        line = jnp.where(lines == index, sums[index], line)
                    squares[0][:, part] = line
        for i in range(tiles):
            out_copy(i).wait()

    any_space = pl.BlockSpec(memory_space=pl.ANY)
    out_shape = [jax.ShapeDtypeStruct((rows, columns), jnp.float32)]
    out_specs = [any_space]
    if spans is not None:
        out_shape.append(jax.ShapeDtypeStruct((8, rows), jnp.float32))
        out_specs.append(pl.BlockSpec(memory_space=pltpu.VMEM))
    operands = [*sum(sources, []), *sum(chunks, [])] + [accumulated] * extra
    needed = 2 * count * depth * (rows + width) + 4 * rows * columns
    results = pl.pallas_call(
        kernel,
        out_shape=out_shape,
        in_specs=[any_space] * len(operands),
        out_specs=out_specs,
        scratch_shapes=[
            pltpu.VMEM((rows, count * depth), sources[0][0].dtype),
            pltpu.VMEM((count * depth, width), chunks[0][0].dtype),
            pltpu.VMEM((rows, columns), jnp.float32),
            pltpu.SemaphoreType.DMA((count, 1 + max(len(block) for block in chunks))),
            pltpu.SemaphoreType.DMA((tiles, 2)),
        ],
        compiler_params=pltpu.CompilerParams(vmem_limit_bytes=needed + 6 * 2**20),
        cost_estimate=pl.CostEstimate(flops=1, bytes_accessed=1, transcendentals=0),
    )(*operands)
    return tuple(results) if spans is not None else results[0]


def attention(total, sums, cosine, sine, starts, query_gain, key_gain, tensor_size, half_rows):
    capacity = total.shape[0]
    q_width, k_width = query_gain.shape[1], key_gain.shape[1]
    heads, kv_heads = q_width // HEAD_DIM, k_width // HEAD_DIM
    group = heads // kv_heads
    block = 128

    def kernel(*refs):
        total_ref, sum_refs = refs[0], refs[1 : 1 + len(sums)]
        cosine_ref, sine_ref, starts_ref, q_gain_ref, k_gain_ref, out_ref = refs[1 + len(sums) :]
        offset = pl.program_id(0) * half_rows
        squares = sum_refs[0][...]
        for other in sum_refs[1:]:
            squares = squares + other[...]
        q_scale = lax.rsqrt(squares[0:1] / (q_width * tensor_size) + EPS)
        k_scale = lax.rsqrt(squares[1:2] / (k_width * tensor_size) + EPS)
        q_scale = jnp.broadcast_to(q_scale, (HEAD_DIM, half_rows)).T
        k_scale = jnp.broadcast_to(k_scale, (HEAD_DIM, half_rows)).T
        cosines, sines = cosine_ref[...], sine_ref[...]

        def rotated(lower, scale, gain):
            field = total_ref[:, lower : lower + HEAD_DIM] * scale * gain
            return (
                field * cosines + pltpu.roll(field, HEAD_DIM // 2, 1) * sines
            ).astype(jnp.bfloat16)

        for g in range(kv_heads):
            low = g * HEAD_DIM
            keys = rotated(q_width + low, k_scale, k_gain_ref[:, low : low + HEAD_DIM])
            values = total_ref[:, q_width + k_width + low : q_width + k_width + low + HEAD_DIM]
            values = values.astype(jnp.bfloat16)
            queries = []
            for h in range(g * group, (g + 1) * group):
                span = slice(h * HEAD_DIM, (h + 1) * HEAD_DIM)
                queries.append(rotated(h * HEAD_DIM, q_scale, q_gain_ref[:, span]))
            for i in range(half_rows // block):
                lower, reach = i * block, (i + 1) * block
                stacked = jnp.concatenate([q[lower:reach] for q in queries], axis=0)
                scores = lax.dot_general(
                    stacked,
                    keys[:reach],
                    (((1,), (1,)), ((), ())),
                    preferred_element_type=jnp.float32,
                ) * (1.0 / math.sqrt(HEAD_DIM))
                first = starts_ref[lower:reach, :] - offset
                lanes = lax.broadcasted_iota(jnp.int32, (block, block), 1)
                row = lax.broadcasted_iota(jnp.int32, (block, block), 0)
                allowed = jnp.concatenate(
                    [lanes + c * block >= first for c in range(i)]
                    + [(lanes + lower >= first) & (lanes <= row)],
                    axis=1,
                )
                scores = scores.reshape(group, block, reach)
                scores = jnp.where(allowed[None], scores, jnp.float32(-1e30))
                peak = jnp.max(scores, axis=-1, keepdims=True)
                expo = jnp.exp(scores - peak)
                probs = expo / jnp.sum(expo, axis=-1, keepdims=True)
                probs = probs.astype(jnp.bfloat16).reshape(group * block, reach)
                mixed = jnp.dot(probs, values[:reach], preferred_element_type=jnp.float32)
                mixed = mixed.astype(jnp.bfloat16)
                for h in range(group):
                    column = (g * group + h) * HEAD_DIM
                    out_ref[lower:reach, column : column + HEAD_DIM] = mixed[
                        h * block : (h + 1) * block
                    ]

    def by_rows(width):
        return pl.BlockSpec((half_rows, width), lambda i: (i, 0))

    def constant(width):
        return pl.BlockSpec((1, width), lambda i: (0, 0))

    return pl.pallas_call(
        kernel,
        grid=(capacity // half_rows,),
        out_shape=jax.ShapeDtypeStruct((capacity, q_width), jnp.bfloat16),
        in_specs=[by_rows(total.shape[1])]
        + [pl.BlockSpec((8, half_rows), lambda i: (0, i))] * len(sums)
        + [by_rows(HEAD_DIM)] * 3
        + [constant(q_width), constant(k_width)],
        out_specs=by_rows(q_width),
        compiler_params=pltpu.CompilerParams(vmem_limit_bytes=24 * 2**20),
        cost_estimate=pl.CostEstimate(flops=1, bytes_accessed=1, transcendentals=0),
    )(total, *sums, cosine, sine, starts, query_gain, key_gain)


def finish(attn_out, sums, tokens, out_gain, live_rows, features):
    rows, width = tokens.shape
    tile = 384 if rows % 384 == 0 else rows

    def kernel(*refs):
        live_ref, attn_ref, sum_refs = refs[0], refs[1], refs[2 : 2 + len(sums)]
        tokens_ref, gain_ref, out_ref = refs[2 + len(sums) :]
        squares = sum_refs[0][...]
        for other in sum_refs[1:]:
            squares = squares + other[...]
        scale = lax.rsqrt(squares[0:1] / features + EPS)
        scale = jnp.broadcast_to(scale, (128, tile)).T
        row = pl.program_id(0) * tile + lax.broadcasted_iota(jnp.int32, (tile, 128), 0)
        live = row < live_ref[0]
        for lower in range(0, width, 128):
            span = slice(lower, lower + 128)
            value = tokens_ref[:, span].astype(jnp.float32) + attn_ref[:, span] * scale * gain_ref[:, span]
            out_ref[:, span] = jnp.where(live, value, 0.0).astype(jnp.bfloat16)

    return pl.pallas_call(
        kernel,
        grid=(rows // tile,),
        out_shape=jax.ShapeDtypeStruct((rows, width), jnp.bfloat16),
        in_specs=[
            pl.BlockSpec(memory_space=pltpu.SMEM),
            pl.BlockSpec((tile, width), lambda i: (i, 0)),
        ]
        + [pl.BlockSpec((8, tile), lambda i: (0, i))] * len(sums)
        + [
            pl.BlockSpec((tile, width), lambda i: (i, 0)),
            pl.BlockSpec((1, width), lambda i: (0, 0)),
        ],
        out_specs=pl.BlockSpec((tile, width), lambda i: (i, 0)),
        compiler_params=pltpu.CompilerParams(vmem_limit_bytes=16 * 2**20),
    )(live_rows, attn_out, *sums, tokens, out_gain)


def body(
    sizes, tokens, live_rows, first_row, w_query, w_key, w_value, w_out, query_gain, key_gain, out_gain
):
    n, tensor_size = sizes
    capacity, width = tokens.shape
    half_rows = capacity // 2
    per_tensor = n // tensor_size

    depth = w_query.shape[0]
    columns = w_query.shape[1] + w_key.shape[1] + w_value.shape[1]
    last = n // 2
    groups = [
        [0] + [offset for step in range(1, last - 1) for offset in (step, n - step)],
        [last - 1, n - last + 1],
        [last],
    ]

    moved = permute(
        w_out,
        sizes,
        lambda f, t: (
            ((f // per_tensor) ^ reverse_bits(t, tensor_size)) * per_tensor + f % per_tensor,
            t,
        ),
    )
    row_ids = jnp.arange(capacity, dtype=jnp.int32)
    positions = (row_ids - first_row).astype(jnp.float32)
    half_dim = HEAD_DIM // 2
    freqs = jnp.power(
        ROPE_BASE, -(jnp.arange(half_dim, dtype=jnp.float32) * 2.0 / HEAD_DIM)
    )
    angle = positions[:, None] * freqs[None, :]
    cosine, sine = jnp.cos(angle), jnp.sin(angle)
    cosine = jnp.concatenate([cosine, cosine], axis=1)
    sine = jnp.concatenate([-sine, sine], axis=1)
    starts = jnp.broadcast_to(first_row[:, None], (capacity, HEAD_DIM))

    weights = jnp.concatenate([w_query, w_key, w_value], axis=1)
    token_blocks = gather_first(tokens, sizes)
    first_ring = ring_open(weights)
    q_width, k_width = w_query.shape[1], w_key.shape[1]

    def choose_tokens(offset):
        block = snake_block(sizes, lax.axis_index("fsdp"), offset)
        which = (block // per_tensor) ^ lax.axis_index("tensor")
        return which, lax.rem(block, per_tensor) * depth, 0

    def qkv_product(number, total):
        return block_product(
            token_blocks,
            choose_tokens,
            {offset: ring_block(first_ring, offset, n) for offset in groups[number]},
            total,
            columns,
            [(0, q_width), (q_width, q_width + k_width)] if number == len(groups) - 1 else None,
        )

    for step in range(1, last - 1):
        ring_step(first_ring, sizes)
        if step == 1:
            token_blocks, moved = ring_tie(first_ring, (token_blocks, moved))
            token_blocks = gather_rest(token_blocks, sizes)
            moved = permute(
                moved, sizes, lambda f, t: (f, (f // per_tensor) ^ reverse_bits(t, tensor_size))
            )
    ring_step(first_ring, sizes)
    total, moved, cosine, sine, starts = ring_tie(
        first_ring, (qkv_product(0, None), moved, cosine, sine, starts)
    )
    ring_middle(first_ring, sizes)
    for number in range(1, len(groups) - 1):
        total = qkv_product(number, total)
    moved, total, _ = lax.optimization_barrier(
        (moved, total, first_ring["middle"])
    )
    total, squares = qkv_product(len(groups) - 1, total)

    second_ring = ring_open(moved)
    ring_step(second_ring, sizes)
    square_blocks = swap_small(squares, sizes)
    attended = attention(
        total,
        square_blocks,
        cosine,
        sine,
        starts,
        query_gain[None, :],
        key_gain[None, :],
        tensor_size,
        half_rows,
    )
    attended_blocks = gather_first(attended, sizes)
    ring_tie(second_ring, attended)

    def choose_attended(offset):
        block = snake_block(sizes, lax.axis_index("fsdp"), offset)
        t_index = lax.axis_index("tensor")
        source = traced_reverse((block // per_tensor) ^ t_index, tensor_size)
        return source ^ t_index, 0, lax.rem(block, per_tensor) * w_out.shape[1]

    def out_product(offsets, sources, attn_out):
        return block_product(
            sources,
            choose_attended,
            {offset: ring_block(second_ring, offset, n) for offset in offsets},
            attn_out,
            width,
            [(0, width)] if last in offsets else None,
        )

    for step in range(2, last - 1):
        ring_step(second_ring, sizes)

    attended_blocks, _ = lax.optimization_barrier(
        (attended_blocks, (second_ring["forward"][-1], second_ring["backward"][-1]))
    )
    attended_blocks = gather_rest(attended_blocks, sizes)
    ring_step(second_ring, sizes)
    attn_out = ring_tie(second_ring, out_product(groups[0], attended_blocks, None))
    ring_middle(second_ring, sizes)
    attn_out = out_product(groups[1], attended_blocks, attn_out)
    attn_out, out_squares = out_product(groups[2], attended_blocks, attn_out)
    return finish(
        attn_out,
        swap_small(out_squares, sizes),
        tokens,
        out_gain[None, :],
        live_rows,
        width * tensor_size,
    )


def solution(mesh):
    sizes = (mesh.shape["fsdp"], mesh.shape["tensor"])

    def run(*arrays):
        return body(sizes, *arrays)

    in_specs = (
        P("fsdp", "tensor"),
        P("fsdp"),
        P("fsdp"),
        P("fsdp", "tensor"),
        P("fsdp", "tensor"),
        P("fsdp", "tensor"),
        P("tensor", "fsdp"),
        P("tensor"),
        P("tensor"),
        P("tensor"),
    )
    return jax.shard_map(
        run, mesh=mesh, in_specs=in_specs, out_specs=P("fsdp", "tensor"), check_vma=False
    )
```

```python
import math

import jax
import jax.numpy as jnp
from jax import lax
from jax.experimental import pallas as pl
from jax.experimental.pallas import tpu as pltpu
from jax.sharding import PartitionSpec as P

HEAD_DIM = 128
EPS = 1e-06
ROPE_BASE = 500000.0
AXES = ("fsdp", "tensor")


def permute(array, mesh_sizes, target):
    n, tensor_size = mesh_sizes
    pairs = []
    for f in range(n):
        for t in range(tensor_size):
            to_f, to_t = target(f, t)
            pairs.append((f * tensor_size + t, to_f * tensor_size + to_t))
    return lax.ppermute(array, AXES, pairs)


def reverse_bits(value, size):
    result = 0
    while size > 1:
        result = result * 2 + value % 2
        value //= 2
        size //= 2
    return result


def snake(n):
    return list(range(0, n, 2)) + list(range(n - 1, 0, -2))


def gather_first(array, sizes):
    half = sizes[1] // 2
    return {0: [array], half: [permute(array, sizes, lambda f, t: (f, t ^ half))]}


def gather_rest(have, sizes):
    bit = sizes[1] // 4
    while bit:
        for r in sorted(have):
            have[r ^ bit] = [
                permute(part, sizes, lambda f, t, bit=bit: (f, t ^ bit)) for part in have[r]
            ]
        bit //= 2
    return [have[r] for r in range(sizes[1])]


def swap_small(array, sizes):
    return [array] + [
        permute(array, sizes, lambda f, t, r=r: (f, t ^ r)) for r in range(1, sizes[1])
    ]


def ring_open(array):
    return {"forward": [array], "backward": [array]}


def ring_send(arrays, sizes):
    n = sizes[0]
    order = snake(n)
    place = {f: i for i, f in enumerate(order)}
    return [
        permute(array, sizes, lambda f, t: (order[(place[f] + way) % n], t))
        for array, way in zip(arrays, (1, -1))
    ]


def ring_step(ring, sizes):
    arrived = ring_send((ring["forward"][-1], ring["backward"][-1]), sizes)
    ring["forward"].append(arrived[0])
    ring["backward"].append(arrived[1])


def ring_middle(ring, sizes):
    forward, backward = ring["forward"][-1], ring["backward"][-1]
    half = forward.shape[0] // 2
    ring["middle"] = ring_send((forward[:half], backward[half:]), sizes)


def ring_tie(ring, other):
    ring["forward"][-1], ring["backward"][-1], other = lax.optimization_barrier(
        (ring["forward"][-1], ring["backward"][-1], other)
    )
    return other


def ring_block(ring, offset, n):
    if 2 * offset == n:
        return ring["middle"]
    block = ring["backward"][offset] if 2 * offset < n else ring["forward"][n - offset]
    return block if isinstance(block, list) else [block]


def snake_block(sizes, f_index, offset):
    n = sizes[0]
    ahead = lax.rem(f_index, 2) == 0
    position = jnp.where(ahead, f_index // 2, n - 1 - f_index // 2)
    place = lax.rem(position + offset, n)
    return jnp.where(place < (n + 1) // 2, 2 * place, 2 * (n - place) - 1)


def traced_reverse(value, size):
    result = value * 0
    while size > 1:
        result = result * 2 + lax.rem(value, 2)
        value = value // 2
        size //= 2
    return result


def block_product(sources, choose, matrices, accumulated, columns, spans):
    rows = sum(part.shape[0] for part in sources[0])
    offsets = list(matrices)
    chunks = [matrices[key] for key in offsets]
    width = chunks[0][0].shape[1]
    depth = sum(chunk.shape[0] for chunk in chunks[0])
    parts = sum(len(block) for block in chunks)
    count = len(chunks)
    if depth % 128 or width % 128:
        stack = jnp.stack([jnp.concatenate(source, axis=0) for source in sources])
        total = jnp.zeros((rows, columns), jnp.float32) if accumulated is None else accumulated
        for j in range(count):
            which, first, column = choose(offsets[j])
            piece = lax.dynamic_slice(stack, (which, 0, first), (1, rows, depth))[0]
            matrix = jnp.concatenate(chunks[j], axis=0)
            term = jnp.dot(piece, matrix, preferred_element_type=jnp.float32)
            current = lax.dynamic_slice(total, (0, column), (rows, width))
            total = lax.dynamic_update_slice(total, current + term, (0, column))
        if spans is None:
            return total
        squares = [jnp.sum(total[:, low:high] ** 2, axis=1) for low, high in spans]
        squares += [jnp.zeros_like(squares[0])] * (8 - len(squares))
        return total, jnp.stack(squares)

    extra = 0 if accumulated is None else 1
    whole = width == columns
    in_place = extra == 1 and not whole and count == 1
    tile = 384 if whole else 256
    tile = tile if rows % tile == 0 else rows
    tiles = rows // tile

    def kernel(*refs):
        held = sum(len(source) for source in sources)
        source, refs = list(refs[:held]), refs[held:]
        source = [[source.pop(0) for _ in each] for each in sources]
        pieces, refs = list(refs[:parts]), refs[parts:]
        pieces = [[pieces.pop(0) for _ in block] for block in chunks]
        start, refs = refs[:extra], refs[extra:]
        out, refs = refs[0], refs[1:]
        squares, refs = refs[: spans is not None], refs[spans is not None :]
        piece, matrix, total, sems, tile_sems = refs
        choices = [choose(offset) for offset in offsets]

        def piece_copy(j, part, lower):
            first = choices[j][1]
            if not isinstance(first, int):
                first = pl.multiple_of(first, 128)
            return pltpu.make_async_copy(
                part.at[:, pl.ds(first, depth)],
                piece.at[pl.ds(lower, part.shape[0]), pl.ds(j * depth, depth)],
                sems.at[j, 0],
            )

        def matrix_copies(j):
            rows_each = depth // len(pieces[j])
            return [
                pltpu.make_async_copy(
                    part,
                    matrix.at[pl.ds(j * depth + k * rows_each, rows_each)],
                    sems.at[j, 1 + k],
                )
                for k, part in enumerate(pieces[j])
            ]

        def in_copy(i):
            part = pl.ds(i * tile, tile)
            return pltpu.make_async_copy(start[0].at[part], total.at[part], tile_sems.at[i, 0])

        def out_copy(i):
            part = pl.ds(i * tile, tile)
            if in_place:
                span = pl.ds(pl.multiple_of(choices[0][2], 128), width)
                return pltpu.make_async_copy(
                    total.at[part, span], out.at[part, span], tile_sems.at[i, 1]
                )
            return pltpu.make_async_copy(total.at[part], out.at[part], tile_sems.at[i, 1])

        for j in range(count):
            for which in range(len(sources)):

                @pl.when(choices[j][0] == which)
                def _(j=j, which=which):
                    lower = 0
                    for part in source[which]:
                        piece_copy(j, part, lower).start()
                        lower += part.shape[0]

            for copy in matrix_copies(j):
                copy.start()
        for i in range(tiles * extra):
            in_copy(i).start()
        together = 2 if whole else 1
        for low in range(0, count, together):
            blocks = range(low, min(low + together, count))
            for j in blocks:
                everything = piece.at[:, pl.ds(j * depth, depth)]
                pltpu.make_async_copy(everything, everything, sems.at[j, 0]).wait()
                for copy in matrix_copies(j):
                    copy.wait()
            span = pl.ds(low * depth, len(blocks) * depth)
            for i in range(tiles):
                part = pl.ds(i * tile, tile)
                if low == 0 and extra:
                    in_copy(i).wait()
                if low == 0 and not extra and not whole:
                    total[part, :] = jnp.zeros((tile, columns), jnp.float32)
                term = jnp.dot(piece[part, span], matrix[span, :], preferred_element_type=jnp.float32)
                if whole:
                    total[part, :] = total[part, :] + term if extra or low else term
                else:
                    total[part, pl.ds(pl.multiple_of(choices[low][2], 128), width)] += term
                if blocks[-1] < count - 1:
                    continue
                out_copy(i).start()
                if spans is not None:
                    sums = []
                    for first, last in spans:
                        chosen = total[part, first:last]
                        chosen = jnp.sum(chosen * chosen, axis=1, keepdims=True)
                        sums.append(jnp.broadcast_to(chosen, (tile, 128)).T[:8])
                    lines = lax.broadcasted_iota(jnp.int32, (8, tile), 0)
                    line = sums[0]
                    for index in range(1, len(sums)):
                        line = jnp.where(lines == index, sums[index], line)
                    squares[0][:, part] = line
        for i in range(tiles):
            out_copy(i).wait()

    any_space = pl.BlockSpec(memory_space=pl.ANY)
    out_shape = [jax.ShapeDtypeStruct((rows, columns), jnp.float32)]
    out_specs = [any_space]
    if spans is not None:
        out_shape.append(jax.ShapeDtypeStruct((8, rows), jnp.float32))
        out_specs.append(pl.BlockSpec(memory_space=pltpu.VMEM))
    operands = [*sum(sources, []), *sum(chunks, [])] + [accumulated] * extra
    needed = 2 * count * depth * (rows + width) + 4 * rows * columns
    results = pl.pallas_call(
        kernel,
        out_shape=out_shape,
        in_specs=[any_space] * len(operands),
        out_specs=out_specs,
        input_output_aliases={len(operands) - 1: 0} if in_place else {},
        scratch_shapes=[
            pltpu.VMEM((rows, count * depth), sources[0][0].dtype),
            pltpu.VMEM((count * depth, width), chunks[0][0].dtype),
            pltpu.VMEM((rows, columns), jnp.float32),
            pltpu.SemaphoreType.DMA((count, 1 + max(len(block) for block in chunks))),
            pltpu.SemaphoreType.DMA((tiles, 2)),
        ],
        compiler_params=pltpu.CompilerParams(vmem_limit_bytes=needed + 6 * 2**20),
        cost_estimate=pl.CostEstimate(flops=1, bytes_accessed=1, transcendentals=0),
    )(*operands)
    return tuple(results) if spans is not None else results[0]


def attention(total, sums, cosine, sine, starts, query_gain, key_gain, tensor_size, half_rows):
    capacity = total.shape[0]
    q_width, k_width = query_gain.shape[1], key_gain.shape[1]
    heads, kv_heads = q_width // HEAD_DIM, k_width // HEAD_DIM
    group = heads // kv_heads
    block = 128

    def kernel(*refs):
        total_ref, sum_refs = refs[0], refs[1 : 1 + len(sums)]
        cosine_ref, sine_ref, starts_ref, q_gain_ref, k_gain_ref, out_ref = refs[1 + len(sums) :]
        offset = pl.program_id(0) * half_rows
        squares = sum_refs[0][...]
        for other in sum_refs[1:]:
            squares = squares + other[...]
        q_scale = lax.rsqrt(squares[0:1] / (q_width * tensor_size) + EPS)
        k_scale = lax.rsqrt(squares[1:2] / (k_width * tensor_size) + EPS)
        q_scale = jnp.broadcast_to(q_scale, (HEAD_DIM, half_rows)).T
        k_scale = jnp.broadcast_to(k_scale, (HEAD_DIM, half_rows)).T
        cosines, sines = cosine_ref[...], sine_ref[...]

        def rotated(lower, scale, gain):
            field = total_ref[:, lower : lower + HEAD_DIM] * scale * gain
            return (
                field * cosines + pltpu.roll(field, HEAD_DIM // 2, 1) * sines
            ).astype(jnp.bfloat16)

        for g in range(kv_heads):
            low = g * HEAD_DIM
            keys = rotated(q_width + low, k_scale, k_gain_ref[:, low : low + HEAD_DIM])
            values = total_ref[:, q_width + k_width + low : q_width + k_width + low + HEAD_DIM]
            values = values.astype(jnp.bfloat16)
            queries = []
            for h in range(g * group, (g + 1) * group):
                span = slice(h * HEAD_DIM, (h + 1) * HEAD_DIM)
                queries.append(rotated(h * HEAD_DIM, q_scale, q_gain_ref[:, span]))
            for i in range(half_rows // block):
                lower, reach = i * block, (i + 1) * block
                stacked = jnp.concatenate([q[lower:reach] for q in queries], axis=0)
                scores = lax.dot_general(
                    stacked,
                    keys[:reach],
                    (((1,), (1,)), ((), ())),
                    preferred_element_type=jnp.float32,
                ) * (1.0 / math.sqrt(HEAD_DIM))
                first = starts_ref[lower:reach, :] - offset
                lanes = lax.broadcasted_iota(jnp.int32, (block, block), 1)
                row = lax.broadcasted_iota(jnp.int32, (block, block), 0)
                allowed = jnp.concatenate(
                    [lanes + c * block >= first for c in range(i)]
                    + [(lanes + lower >= first) & (lanes <= row)],
                    axis=1,
                )
                scores = scores.reshape(group, block, reach)
                scores = jnp.where(allowed[None], scores, jnp.float32(-1e30))
                peak = jnp.max(scores, axis=-1, keepdims=True)
                expo = jnp.exp(scores - peak)
                probs = expo / jnp.sum(expo, axis=-1, keepdims=True)
                probs = probs.astype(jnp.bfloat16).reshape(group * block, reach)
                mixed = jnp.dot(probs, values[:reach], preferred_element_type=jnp.float32)
                mixed = mixed.astype(jnp.bfloat16)
                for h in range(group):
                    column = (g * group + h) * HEAD_DIM
                    out_ref[lower:reach, column : column + HEAD_DIM] = mixed[
                        h * block : (h + 1) * block
                    ]

    def by_rows(width):
        return pl.BlockSpec((half_rows, width), lambda i: (i, 0))

    def constant(width):
        return pl.BlockSpec((1, width), lambda i: (0, 0))

    return pl.pallas_call(
        kernel,
        grid=(capacity // half_rows,),
        out_shape=jax.ShapeDtypeStruct((capacity, q_width), jnp.bfloat16),
        in_specs=[by_rows(total.shape[1])]
        + [pl.BlockSpec((8, half_rows), lambda i: (0, i))] * len(sums)
        + [by_rows(HEAD_DIM)] * 3
        + [constant(q_width), constant(k_width)],
        out_specs=by_rows(q_width),
        compiler_params=pltpu.CompilerParams(vmem_limit_bytes=24 * 2**20),
        cost_estimate=pl.CostEstimate(flops=1, bytes_accessed=1, transcendentals=0),
    )(total, *sums, cosine, sine, starts, query_gain, key_gain)


def finish(attn_out, sums, tokens, out_gain, live_rows, features):
    rows, width = tokens.shape
    tile = 384 if rows % 384 == 0 else rows

    def kernel(*refs):
        live_ref, attn_ref, sum_refs = refs[0], refs[1], refs[2 : 2 + len(sums)]
        tokens_ref, gain_ref, out_ref = refs[2 + len(sums) :]
        squares = sum_refs[0][...]
        for other in sum_refs[1:]:
            squares = squares + other[...]
        scale = lax.rsqrt(squares[0:1] / features + EPS)
        scale = jnp.broadcast_to(scale, (128, tile)).T
        row = pl.program_id(0) * tile + lax.broadcasted_iota(jnp.int32, (tile, 128), 0)
        live = row < live_ref[0]
        for lower in range(0, width, 128):
            span = slice(lower, lower + 128)
            value = tokens_ref[:, span].astype(jnp.float32) + attn_ref[:, span] * scale * gain_ref[:, span]
            out_ref[:, span] = jnp.where(live, value, 0.0).astype(jnp.bfloat16)

    return pl.pallas_call(
        kernel,
        grid=(rows // tile,),
        out_shape=jax.ShapeDtypeStruct((rows, width), jnp.bfloat16),
        in_specs=[
            pl.BlockSpec(memory_space=pltpu.SMEM),
            pl.BlockSpec((tile, width), lambda i: (i, 0)),
        ]
        + [pl.BlockSpec((8, tile), lambda i: (0, i))] * len(sums)
        + [
            pl.BlockSpec((tile, width), lambda i: (i, 0)),
            pl.BlockSpec((1, width), lambda i: (0, 0)),
        ],
        out_specs=pl.BlockSpec((tile, width), lambda i: (i, 0)),
        compiler_params=pltpu.CompilerParams(vmem_limit_bytes=16 * 2**20),
    )(live_rows, attn_out, *sums, tokens, out_gain)


def body(
    sizes, tokens, live_rows, first_row, w_query, w_key, w_value, w_out, query_gain, key_gain, out_gain
):
    n, tensor_size = sizes
    capacity, width = tokens.shape
    half_rows = capacity // 2
    per_tensor = n // tensor_size

    depth = w_query.shape[0]
    columns = w_query.shape[1] + w_key.shape[1] + w_value.shape[1]
    last = n // 2
    groups = [
        [0] + [offset for step in range(1, last - 1) for offset in (step, n - step)],
        [last - 1, n - last + 1],
        [last],
    ]

    moved = permute(
        w_out,
        sizes,
        lambda f, t: (
            ((f // per_tensor) ^ reverse_bits(t, tensor_size)) * per_tensor + f % per_tensor,
            t,
        ),
    )
    row_ids = jnp.arange(capacity, dtype=jnp.int32)
    positions = (row_ids - first_row).astype(jnp.float32)
    half_dim = HEAD_DIM // 2
    freqs = jnp.power(
        ROPE_BASE, -(jnp.arange(half_dim, dtype=jnp.float32) * 2.0 / HEAD_DIM)
    )
    angle = positions[:, None] * freqs[None, :]
    cosine, sine = jnp.cos(angle), jnp.sin(angle)
    cosine = jnp.concatenate([cosine, cosine], axis=1)
    sine = jnp.concatenate([-sine, sine], axis=1)
    starts = jnp.broadcast_to(first_row[:, None], (capacity, HEAD_DIM))

    weights = jnp.concatenate([w_query, w_key, w_value], axis=1)
    token_blocks = gather_first(tokens, sizes)
    first_ring = ring_open(weights)
    q_width, k_width = w_query.shape[1], w_key.shape[1]

    def choose_tokens(offset):
        block = snake_block(sizes, lax.axis_index("fsdp"), offset)
        which = (block // per_tensor) ^ lax.axis_index("tensor")
        return which, lax.rem(block, per_tensor) * depth, 0

    def qkv_product(number, total):
        return block_product(
            token_blocks,
            choose_tokens,
            {offset: ring_block(first_ring, offset, n) for offset in groups[number]},
            total,
            columns,
            [(0, q_width), (q_width, q_width + k_width)] if number == len(groups) - 1 else None,
        )

    for step in range(1, last - 1):
        ring_step(first_ring, sizes)
        if step == 1:
            token_blocks, moved = ring_tie(first_ring, (token_blocks, moved))
            token_blocks = gather_rest(token_blocks, sizes)
            moved = permute(
                moved, sizes, lambda f, t: (f, (f // per_tensor) ^ reverse_bits(t, tensor_size))
            )
    ring_step(first_ring, sizes)
    total, moved, cosine, sine, starts = ring_tie(
        first_ring, (qkv_product(0, None), moved, cosine, sine, starts)
    )
    ring_middle(first_ring, sizes)
    for number in range(1, len(groups) - 1):
        total = qkv_product(number, total)
    moved, total, _ = lax.optimization_barrier(
        (moved, total, first_ring["middle"])
    )
    total, squares = qkv_product(len(groups) - 1, total)

    second_ring = ring_open(moved)
    ring_step(second_ring, sizes)
    square_blocks = swap_small(squares, sizes)
    attended = attention(
        total,
        square_blocks,
        cosine,
        sine,
        starts,
        query_gain[None, :],
        key_gain[None, :],
        tensor_size,
        half_rows,
    )
    attended_blocks = gather_first(attended, sizes)
    ring_tie(second_ring, attended)

    def choose_attended(offset):
        block = snake_block(sizes, lax.axis_index("fsdp"), offset)
        t_index = lax.axis_index("tensor")
        source = traced_reverse((block // per_tensor) ^ t_index, tensor_size)
        return source ^ t_index, 0, lax.rem(block, per_tensor) * w_out.shape[1]

    def out_product(offsets, sources, attn_out):
        return block_product(
            sources,
            choose_attended,
            {offset: ring_block(second_ring, offset, n) for offset in offsets},
            attn_out,
            width,
            [(0, width)] if last in offsets else None,
        )

    for step in range(2, last - 1):
        ring_step(second_ring, sizes)

    attended_blocks, _ = lax.optimization_barrier(
        (attended_blocks, (second_ring["forward"][-1], second_ring["backward"][-1]))
    )
    attended_blocks = gather_rest(attended_blocks, sizes)
    ring_step(second_ring, sizes)
    attn_out = ring_tie(second_ring, out_product(groups[0], attended_blocks, None))
    ring_middle(second_ring, sizes)
    attn_out = out_product(groups[1], attended_blocks, attn_out)
    attn_out, out_squares = out_product(groups[2], attended_blocks, attn_out)
    return finish(
        attn_out,
        swap_small(out_squares, sizes),
        tokens,
        out_gain[None, :],
        live_rows,
        width * tensor_size,
    )


def solution(mesh):
    sizes = (mesh.shape["fsdp"], mesh.shape["tensor"])

    def run(*arrays):
        return body(sizes, *arrays)

    in_specs = (
        P("fsdp", "tensor"),
        P("fsdp"),
        P("fsdp"),
        P("fsdp", "tensor"),
        P("fsdp", "tensor"),
        P("fsdp", "tensor"),
        P("tensor", "fsdp"),
        P("tensor"),
        P("tensor"),
        P("tensor"),
    )
    return jax.shard_map(
        run, mesh=mesh, in_specs=in_specs, out_specs=P("fsdp", "tensor"), check_vma=False
    )
```
